512 devices in a mesh: seq: 64 (over x, z, core), chan: 8 (over y).
Axes of the slice: x: 4, y: 8, z: 8, core: 2. Of those that a mesh axis runs over, the one named last changes fastest.
Arguments:
- projections: bfloat16 [3, 256, 32768], P(None, 'chan', 'seq'), may hold values from -6 to 6
- short_weight: float32 [3, 256, 3], P(None, 'chan'), may hold values from -3.5 to 3.5
- long_filter: bfloat16 [256, 32768], P('chan', 'seq'), may hold values from -0.03125 to 0.03125
- skip_gain: float32 [256], P('chan'), may hold values from 0.5 to 1.5
Outputs:
- gated: bfloat16 [256, 32768], P('chan', 'seq')
The draws below stay inside these ranges and needn't reach their ends.
All inputs are finite; a program needn't handle non-finite values.
Results may differ from the reference program's by a relative error of at most 0.011.
Values may be sent and summed in bfloat16 or wider, within the bound.
A program may use at most 64 MiB of HBM per device.

```python
import jax
import jax.numpy as jnp
from jax import lax

C = 256
TOKENS = 32768


def block_scale(key, shape, cuts, low, largest):
    gain = 1.0
    for dim, shards_of in cuts:
        draws = jax.random.uniform(jax.random.fold_in(jax.random.fold_in(key, 6), dim), (shards_of,), jnp.float32, low / len(cuts), largest / len(cuts))
        gain = gain * jnp.repeat(jnp.exp(draws), shape[dim] // shards_of).reshape((-1,) + (1,) * (len(shape) - 1 - dim))
    return gain


def scatter_about(stream_key, dims, scale, limit, shards=(), held_as=jnp.bfloat16):
    drawn = scale * jax.random.normal(stream_key, dims, jnp.float32)
    if shards:
        drawn = drawn * block_scale(stream_key, dims, shards, -0.22, 0.18)
    return jnp.clip(drawn, -limit, limit).astype(held_as)


def setup_inputs(seed: int = 0) -> dict:
    keys = jax.random.split(jax.random.key(seed), 5)
    return {
        "projections": scatter_about(keys[0], (3, C, TOKENS), 1.0, 6.0, ((1, 8), (2, 64))),
        "short_weight": scatter_about(keys[1], (3, C, 3), 3 ** -0.5, 3.5, ((1, 8),), jnp.float32),
        "long_filter": scatter_about(keys[2], (C, TOKENS), TOKENS ** -0.5, 0.03125, ((0, 8), (1, 64))),
        "skip_gain": jnp.clip(0.5 + 1.0 * jax.random.uniform(keys[3], (C,), jnp.float32) ** block_scale(keys[3], (C,), ((0, 8),), -0.2, 0.2), 0.5, 1.5),
    }


def long_row(pair):
    signal, taps = pair
    spectrum = jnp.fft.rfft(signal, n=2 * TOKENS) * jnp.fft.rfft(taps, n=2 * TOKENS)
    return jnp.fft.irfft(spectrum, n=2 * TOKENS)[:TOKENS].astype(jnp.float32)


def reference(projections, short_weight, long_filter, skip_gain):
    padded = jnp.pad(projections.astype(jnp.float32), ((0, 0), (0, 0), (2, 0)))
    conv = short_weight[:, :, 0:1] * padded[:, :, :TOKENS]
    conv = conv + short_weight[:, :, 1:2] * padded[:, :, 1:TOKENS + 1]
    conv = conv + short_weight[:, :, 2:3] * padded[:, :, 2:]
    conv = conv.astype(jnp.bfloat16)
    query = conv[0].astype(jnp.float32)
    mixed_in = (conv[1].astype(jnp.float32) * conv[2].astype(jnp.float32)).astype(jnp.bfloat16)
    long_out = lax.map(long_row, (mixed_in.astype(jnp.float32), long_filter.astype(jnp.float32)))
    gated = query * (long_out + skip_gain[:, None] * mixed_in.astype(jnp.float32))
    return gated.astype(jnp.bfloat16)
```

```python
import functools

import jax
import jax.numpy as jnp
import numpy as np
from jax import lax
from jax.experimental import pallas as pl
from jax.experimental.pallas import tpu as pltpu
from jax.sharding import PartitionSpec as P

MESH = pl.DeviceIdType.MESH
LANES = 128
f32 = jnp.float32
bf16 = jnp.bfloat16


def tables(blocks, pieces):
    rows = blocks * pieces
    n = rows * LANES
    order = (np.arange(blocks)[None, :] * pieces + np.arange(pieces)[:, None]).reshape(-1)
    k1 = np.arange(rows) + 0.25
    first = np.exp(-2j * np.pi * np.outer(k1, order) / rows)
    turn = np.exp(-2j * np.pi * np.outer(k1, np.arange(LANES)) / n)
    second = np.exp(-2j * np.pi * np.outer(np.arange(LANES), np.arange(LANES)) / LANES)
    back = np.conj(second)
    last = np.conj(first).T / n
    w1 = np.concatenate([first.real, first.imag], 0)
    w3 = np.block([[second.real, second.imag], [-second.imag, second.real]])
    w4 = np.block([[back.real, back.imag], [-back.imag, back.real]])
    w6 = np.concatenate([last.real, -last.imag], 1)
    tw = np.stack([turn.real, turn.imag])
    return tuple(x.astype(np.float32) for x in (w1, w3, w4, w6, tw))


def dot(a, b):
    return jnp.dot(a, b, preferred_element_type=f32)


def kernel(
    blocks, proj, weight, filt, gain, w1, w3, w4, w6, tw, out,
    proj_v, filt_v, weight_v, gain_s, w1_v, w3_v, w4_v, w6_v, tw_v,
    spread, msg, inbox, opened, result, back, out_v,
    load_sem, const_sem, send_sem, recv_sem, send2_sem, recv2_sem,
):
    chips = blocks // 2
    chans = proj.shape[1]
    pieces = proj.shape[2] // LANES
    me = lax.axis_index("seq")
    chip = me // 2
    core = lax.rem(me, 2)
    first_core = core == 0
    loads = [
        pltpu.make_async_copy(proj, proj_v, load_sem.at[0]),
        pltpu.make_async_copy(filt, filt_v, load_sem.at[1]),
    ]
    for load in loads:
        load.start()
    consts = [
        pltpu.make_async_copy(src, dst, const_sem.at[i])
        for i, (src, dst) in enumerate(
            [(w1, w1_v), (w3, w3_v), (w4, w4_v), (w6, w6_v), (tw, tw_v), (weight, weight_v), (gain, gain_s)]
        )
    ]

    barrier = pltpu.get_barrier_semaphore()

    @pl.when(first_core)
    def _():
        def greet(i, carry):
            pl.semaphore_signal(
                barrier, inc=1, device_id={"seq": lax.rem(me + i, blocks)}, device_id_type=MESH
            )
            return carry

        lax.fori_loop(1, blocks, greet, 0)

    @pl.when(core == 1)
    def _():
        def greet(i, carry):
            pl.semaphore_signal(
                barrier, inc=1, device_id={"seq": 2 * lax.rem(chip + i, chips)}, device_id_type=MESH
            )
            return carry

        lax.fori_loop(0, chips, greet, 0)

    @pl.when(first_core)
    def _():
        for const in consts:
            const.start()

    for load in loads:
        load.wait()
    for j in range(4):
        for r in range(pieces):
            cols = slice(LANES * r, LANES * (r + 1))
            piece = proj_v[j, :, cols] if j < 3 else filt_v[:, cols]
            spread[pl.ds(j * pieces + r, chans, stride=4 * pieces), :] = piece.astype(f32)
    msg[...] = spread[...].reshape(chans, 4 * pieces, LANES).astype(bf16)

    @pl.when(first_core)
    def _():
        pl.semaphore_wait(barrier, blocks - 1)

    @pl.when(core == 1)
    def _():
        pl.semaphore_wait(barrier, chips)

    def send(i, carry):
        p = lax.rem(chip + i, chips)
        pltpu.make_async_remote_copy(
            src_ref=msg.at[p],
            dst_ref=inbox.at[me],
            send_sem=send_sem,
            recv_sem=recv_sem,
            device_id={"seq": 2 * p},
            device_id_type=MESH,
        ).start()
        return carry

    @pl.when(core == 1)
    def _():
        send(0, 0)

    lax.fori_loop(1, chips, send, 0)

    @pl.when(first_core)
    def _():
        inbox[me] = msg[chip]
        for const in consts:
            const.wait()
        others = inbox.at[pl.ds(0, blocks - 1)]
        pltpu.make_async_copy(others, others, recv_sem).wait()
        opened[...] = inbox[...].astype(f32).reshape(blocks * 4 * pieces, LANES)
        part = [
            [opened[pl.ds(j * pieces + r, blocks, stride=4 * pieces), :] for r in range(pieces)]
            for j in range(4)
        ]
        lane = lax.broadcasted_iota(jnp.int32, (blocks, LANES), 1)
        row = lax.broadcasted_iota(jnp.int32, (blocks, LANES), 0)
        chan_lane = lax.broadcasted_iota(jnp.int32, weight_v.shape[1:], 1)
        conv = []
        for j in range(3):
            taps = jnp.sum(jnp.where(chan_lane == chip, weight_v[j], 0.0), axis=1, keepdims=True)
            before = jnp.where(row == 0, 0.0, pltpu.roll(part[j][pieces - 1], 1, 0))
            done = []
            for r in range(pieces):
                now = part[j][r]
                one = pltpu.roll(jnp.where(lane >= LANES - 1, before, now), 1, 1)
                two = pltpu.roll(jnp.where(lane >= LANES - 2, before, now), 2, 1)
                total = taps[0:1, :] * two
                total = total + taps[1:2, :] * one
                total = total + taps[2:3, :] * now
                done.append(total.astype(bf16).astype(f32))
                before = now
            conv.append(jnp.concatenate(done, 0))
        query, key, value = conv
        mixed = (key * value).astype(bf16)
        taps = jnp.concatenate(part[3], 0).astype(bf16)
        rows = blocks * pieces
        both = jnp.concatenate([mixed, taps], 1)
        step = dot(w1_v[...].astype(bf16), both)
        tr, ti = tw_v[0], tw_v[1]
        turned = []
        for half in (slice(0, LANES), slice(LANES, 2 * LANES)):
            re, im = step[:rows, half], step[rows:, half]
            turned.append(jnp.concatenate([re * tr - im * ti, re * ti + im * tr], 1).astype(bf16))
        spec = dot(jnp.concatenate(turned, 0), w3_v[...].astype(bf16))
        xr, xi = spec[:rows, :LANES], spec[:rows, LANES:]
        hr, hi = spec[rows:, :LANES], spec[rows:, LANES:]
        prod = jnp.concatenate([xr * hr - xi * hi, xr * hi + xi * hr], 1).astype(bf16)
        inv = dot(prod, w4_v[...].astype(bf16))
        re, im = inv[:, :LANES], inv[:, LANES:]
        untwist = jnp.concatenate([re * tr + im * ti, im * tr - re * ti], 0).astype(bf16)
        long_out = dot(w6_v[...].astype(bf16), untwist)
        gated = query * (long_out + gain_s[chip] * mixed.astype(f32))
        for r in range(pieces):
            result[pl.ds(r, blocks, stride=pieces), :] = gated[r * blocks : (r + 1) * blocks]
        back[chip] = result[pl.ds(pl.multiple_of(me * pieces, pieces), pieces), :]

        def reply(i, carry):
            a = lax.rem(me + i, blocks)
            pltpu.make_async_remote_copy(
                src_ref=result.at[pl.ds(pl.multiple_of(a * pieces, pieces), pieces), :],
                dst_ref=back.at[chip],
                send_sem=send2_sem,
                recv_sem=recv2_sem,
                device_id={"seq": a},
                device_id_type=MESH,
            ).start()
            return carry

        lax.fori_loop(1, blocks, reply, 0)
        mine = back.at[pl.ds(0, chips - 1)]
        pltpu.make_async_copy(mine, mine, recv2_sem).wait()

    @pl.when(core == 1)
    def _():
        pltpu.make_async_copy(back, back, recv2_sem).wait()

    for r in range(pieces):
        out_v[:, LANES * r : LANES * (r + 1)] = back[:, r, :].astype(bf16)
    store = pltpu.make_async_copy(out_v, out, load_sem.at[2])
    store.start()

    @pl.when(first_core)
    def _():
        sent = msg.at[pl.ds(0, chips - 1)]
        pltpu.make_async_copy(sent, sent, send_sem).wait()
        sent = result.at[pl.ds(0, (blocks - 1) * pieces), :]
        pltpu.make_async_copy(sent, sent, send2_sem).wait()

    @pl.when(core == 1)
    def _():
        pltpu.make_async_copy(msg, msg, send_sem).wait()

    store.wait()


def shards(blocks, projections, short_weight, long_filter, skip_gain):
    _, chans, tokens = projections.shape
    pieces = tokens // LANES
    rows = blocks * pieces
    consts = [jnp.asarray(x) for x in tables(blocks, pieces)]
    weight = jnp.transpose(short_weight, (0, 2, 1))
    dma = pltpu.SemaphoreType.DMA
    scratch = [
        pltpu.VMEM(projections.shape, bf16),
        pltpu.VMEM(long_filter.shape, bf16),
        pltpu.VMEM(weight.shape, f32),
        pltpu.SMEM(skip_gain.shape, f32),
        *[pltpu.VMEM(x.shape, x.dtype) for x in consts],
        pltpu.VMEM((chans * 4 * pieces, LANES), f32),
        pltpu.VMEM((chans, 4 * pieces, LANES), bf16),
        pltpu.VMEM((blocks, 4 * pieces, LANES), bf16),
        pltpu.VMEM((blocks * 4 * pieces, LANES), f32),
        pltpu.VMEM((rows, LANES), f32),
        pltpu.VMEM((chans, pieces, LANES), f32),
        pltpu.VMEM((chans, tokens), bf16),
        dma((3,)), dma((7,)), dma, dma, dma, dma,
    ]
    return pl.pallas_call(
        functools.partial(kernel, blocks),
        out_shape=jax.ShapeDtypeStruct((chans, tokens), bf16),
        in_specs=[pl.BlockSpec(memory_space=pl.ANY)] * 9,
        out_specs=pl.BlockSpec(memory_space=pl.ANY),
        scratch_shapes=scratch,
        compiler_params=pltpu.CompilerParams(
            collective_id=0, has_side_effects=True, vmem_limit_bytes=56 * 1024 * 1024
        ),
        cost_estimate=pl.CostEstimate(flops=200_000_000, bytes_accessed=2_000_000, transcendentals=0),
        name="hyena",
    )(projections, weight, long_filter, skip_gain, *consts)


def solution(mesh):
    in_specs = (P(None, "chan", "seq"), P(None, "chan", None), P("chan", "seq"), P("chan"))
    out_specs = P("chan", "seq")
    body = functools.partial(shards, mesh.shape["seq"])
    return jax.shard_map(body, mesh=mesh, in_specs=in_specs, out_specs=out_specs, check_vma=False)
```

```python
import functools

import jax
import jax.numpy as jnp
import numpy as np
from jax import lax
from jax.experimental import pallas as pl
from jax.experimental.pallas import tpu as pltpu
from jax.sharding import PartitionSpec as P

MESH = pl.DeviceIdType.MESH
LANES = 128
GROUP = 8
f32 = jnp.float32
bf16 = jnp.bfloat16


def tables(blocks, pieces):
    rows = blocks * pieces
    n = rows * LANES
    order = (np.arange(blocks)[None, :] * pieces + np.arange(pieces)[:, None]).reshape(-1)
    k1 = np.arange(rows) + 0.25
    first = np.exp(-2j * np.pi * np.outer(k1, order) / rows)
    turn = np.exp(-2j * np.pi * np.outer(k1, np.arange(LANES)) / n)
    second = np.exp(-2j * np.pi * np.outer(np.arange(LANES), np.arange(LANES)) / LANES)
    back = np.conj(second)
    last = np.conj(first).T / n
    w1 = np.concatenate([first.real, first.imag], 0)
    w3 = np.block([[second.real, second.imag], [-second.imag, second.real]])
    w4 = np.block([[back.real, back.imag], [-back.imag, back.real]])
    w6 = np.concatenate([last.real, -last.imag], 1)
    tw = np.stack([turn.real, turn.imag])
    return tuple(x.astype(np.float32) for x in (w1, w3, w4, w6, tw))


def dot(a, b):
    return jnp.dot(a, b, preferred_element_type=f32)


def kernel(
    blocks, proj, weight, filt, gain, w1, w3, w4, w6, tw, out,
    proj_v, filt_v, weight_v, gain_s, w1_v, w3_v, w4_v, w6_v, tw_v,
    spread, msg, inbox, opened, result, back, out_v,
    load_sem, const_sem, send_sem, recv_sem, send2_sem, recv2_sem,
):
    chans = proj.shape[1]
    pieces = proj.shape[2] // LANES
    me = lax.axis_index("seq")
    group, place = me // (2 * GROUP), lax.rem(me, 2 * GROUP)
    holder = place < GROUP
    mine = group * GROUP + lax.rem(place, GROUP)

    def home(ch):
        return (ch // GROUP) * (2 * GROUP) + lax.rem(ch, GROUP)

    loads = [
        pltpu.make_async_copy(proj, proj_v, load_sem.at[0]),
        pltpu.make_async_copy(filt, filt_v, load_sem.at[1]),
    ]
    for load in loads:
        load.start()
    consts = [
        pltpu.make_async_copy(src, dst, const_sem.at[i])
        for i, (src, dst) in enumerate(
            [(w1, w1_v), (w3, w3_v), (w4, w4_v), (w6, w6_v), (tw, tw_v), (weight, weight_v), (gain, gain_s)]
        )
    ]

    barrier = pltpu.get_barrier_semaphore()

    @pl.when(holder)
    def _():
        def greet(i, carry):
            pl.semaphore_signal(
                barrier, inc=1, device_id={"seq": lax.rem(me + i, blocks)}, device_id_type=MESH
            )
            return carry

        lax.fori_loop(1, blocks, greet, 0)
        for const in consts:
            const.start()

    for load in loads:
        load.wait()
    for j in range(4):
        for r in range(pieces):
            cols = slice(LANES * r, LANES * (r + 1))
            piece = proj_v[j, :, cols] if j < 3 else filt_v[:, cols]
            spread[pl.ds(j * pieces + r, chans, stride=4 * pieces), :] = piece.astype(f32)
    msg[...] = spread[...].reshape(chans, 4 * pieces, LANES).astype(bf16)

    @pl.when(holder)
    def _():
        pl.semaphore_wait(barrier, chans - 1)

    @pl.when(jnp.logical_not(holder))
    def _():
        pl.semaphore_wait(barrier, chans)

    def send(i, carry):
        ch = lax.rem(mine + i, chans)
        pltpu.make_async_remote_copy(
            src_ref=msg.at[ch],
            dst_ref=inbox.at[me],
            send_sem=send_sem,
            recv_sem=recv_sem,
            device_id={"seq": home(ch)},
            device_id_type=MESH,
        ).start()
        return carry

    @pl.when(jnp.logical_not(holder))
    def _():
        send(0, 0)

    lax.fori_loop(1, chans, send, 0)

    @pl.when(holder)
    def _():
        inbox[me] = msg[mine]
        for const in consts:
            const.wait()
        others = inbox.at[pl.ds(0, blocks - 1)]
        pltpu.make_async_copy(others, others, recv_sem).wait()
        opened[...] = inbox[...].astype(f32).reshape(blocks * 4 * pieces, LANES)
        part = [
            [opened[pl.ds(j * pieces + r, blocks, stride=4 * pieces), :] for r in range(pieces)]
            for j in range(4)
        ]
        lane = lax.broadcasted_iota(jnp.int32, (blocks, LANES), 1)
        row = lax.broadcasted_iota(jnp.int32, (blocks, LANES), 0)
        chan_lane = lax.broadcasted_iota(jnp.int32, weight_v.shape[1:], 1)
        conv = []
        for j in range(3):
            taps = jnp.sum(jnp.where(chan_lane == mine, weight_v[j], 0.0), axis=1, keepdims=True)
            before = jnp.where(row == 0, 0.0, pltpu.roll(part[j][pieces - 1], 1, 0))
            done = []
            for r in range(pieces):
                now = part[j][r]
                one = pltpu.roll(jnp.where(lane >= LANES - 1, before, now), 1, 1)
                two = pltpu.roll(jnp.where(lane >= LANES - 2, before, now), 2, 1)
                total = taps[0:1, :] * two
                total = total + taps[1:2, :] * one
                total = total + taps[2:3, :] * now
                done.append(total.astype(bf16).astype(f32))
                before = now
            conv.append(jnp.concatenate(done, 0))
        query, key, value = conv
        mixed = (key * value).astype(bf16)
        taps = jnp.concatenate(part[3], 0).astype(bf16)
        rows = blocks * pieces
        both = jnp.concatenate([mixed, taps], 1)
        step = dot(w1_v[...].astype(bf16), both)
        tr, ti = tw_v[0], tw_v[1]
        turned = []
        for half in (slice(0, LANES), slice(LANES, 2 * LANES)):
            re, im = step[:rows, half], step[rows:, half]
            turned.append(jnp.concatenate([re * tr - im * ti, re * ti + im * tr], 1).astype(bf16))
        spec = dot(jnp.concatenate(turned, 0), w3_v[...].astype(bf16))
        xr, xi = spec[:rows, :LANES], spec[:rows, LANES:]
        hr, hi = spec[rows:, :LANES], spec[rows:, LANES:]
        prod = jnp.concatenate([xr * hr - xi * hi, xr * hi + xi * hr], 1).astype(bf16)
        inv = dot(prod, w4_v[...].astype(bf16))
        re, im = inv[:, :LANES], inv[:, LANES:]
        untwist = jnp.concatenate([re * tr + im * ti, im * tr - re * ti], 0).astype(bf16)
        long_out = dot(w6_v[...].astype(bf16), untwist)
        gated = query * (long_out + gain_s[mine] * mixed.astype(f32))
        for r in range(pieces):
            result[pl.ds(r, blocks, stride=pieces), :] = gated[r * blocks : (r + 1) * blocks]
        back[mine] = result[pl.ds(pl.multiple_of(me * pieces, pieces), pieces), :]

        def reply(i, carry):
            a = lax.rem(me + i, blocks)
            pltpu.make_async_remote_copy(
                src_ref=result.at[pl.ds(pl.multiple_of(a * pieces, pieces), pieces), :],
                dst_ref=back.at[mine],
                send_sem=send2_sem,
                recv_sem=recv2_sem,
                device_id={"seq": a},
                device_id_type=MESH,
            ).start()
            return carry

        lax.fori_loop(1, blocks, reply, 0)
        others = back.at[pl.ds(0, chans - 1)]
        pltpu.make_async_copy(others, others, recv2_sem).wait()

    @pl.when(jnp.logical_not(holder))
    def _():
        pltpu.make_async_copy(back, back, recv2_sem).wait()

    for r in range(pieces):
        out_v[:, LANES * r : LANES * (r + 1)] = back[:, r, :].astype(bf16)
    store = pltpu.make_async_copy(out_v, out, load_sem.at[2])
    store.start()

    @pl.when(holder)
    def _():
        sent = msg.at[pl.ds(0, chans - 1)]
        pltpu.make_async_copy(sent, sent, send_sem).wait()
        sent = result.at[pl.ds(0, (blocks - 1) * pieces), :]
        pltpu.make_async_copy(sent, sent, send2_sem).wait()

    @pl.when(jnp.logical_not(holder))
    def _():
        pltpu.make_async_copy(msg, msg, send_sem).wait()

    store.wait()


def shards(blocks, projections, short_weight, long_filter, skip_gain):
    _, chans, tokens = projections.shape
    pieces = tokens // LANES
    rows = blocks * pieces
    consts = [jnp.asarray(x) for x in tables(blocks, pieces)]
    weight = jnp.transpose(short_weight, (0, 2, 1))
    dma = pltpu.SemaphoreType.DMA
    scratch = [
        pltpu.VMEM(projections.shape, bf16),
        pltpu.VMEM(long_filter.shape, bf16),
        pltpu.VMEM(weight.shape, f32),
        pltpu.SMEM(skip_gain.shape, f32),
        *[pltpu.VMEM(x.shape, x.dtype) for x in consts],
        pltpu.VMEM((chans * 4 * pieces, LANES), f32),
        pltpu.VMEM((chans, 4 * pieces, LANES), bf16),
        pltpu.VMEM((blocks, 4 * pieces, LANES), bf16),
        pltpu.VMEM((blocks * 4 * pieces, LANES), f32),
        pltpu.VMEM((rows, LANES), f32),
        pltpu.VMEM((chans, pieces, LANES), f32),
        pltpu.VMEM((chans, tokens), bf16),
        dma((3,)), dma((7,)), dma, dma, dma, dma,
    ]
    return pl.pallas_call(
        functools.partial(kernel, blocks),
        out_shape=jax.ShapeDtypeStruct((chans, tokens), bf16),
        in_specs=[pl.BlockSpec(memory_space=pl.ANY)] * 9,
        out_specs=pl.BlockSpec(memory_space=pl.ANY),
        scratch_shapes=scratch,
        compiler_params=pltpu.CompilerParams(
            collective_id=0, has_side_effects=True, vmem_limit_bytes=56 * 1024 * 1024
        ),
        cost_estimate=pl.CostEstimate(flops=200_000_000, bytes_accessed=2_000_000, transcendentals=0),
        name="hyena",
    )(projections, weight, long_filter, skip_gain, *consts)


def solution(mesh):
    in_specs = (P(None, "chan", "seq"), P(None, "chan", None), P("chan", "seq"), P("chan"))
    out_specs = P("chan", "seq")
    body = functools.partial(shards, mesh.shape["seq"])
    return jax.shard_map(body, mesh=mesh, in_specs=in_specs, out_specs=out_specs, check_vma=False)
```

```python
import functools

import jax
import jax.numpy as jnp
import numpy as np
from jax import lax
from jax.experimental import pallas as pl
from jax.experimental.pallas import tpu as pltpu
from jax.sharding import PartitionSpec as P

MESH = pl.DeviceIdType.MESH
LANES = 128
GROUP = 8
f32 = jnp.float32
bf16 = jnp.bfloat16


def tables(blocks, pieces):
    rows = blocks * pieces
    n = rows * LANES
    order = (np.arange(blocks)[None, :] * pieces + np.arange(pieces)[:, None]).reshape(-1)
    k1 = np.arange(rows) + 0.25
    first = np.exp(-2j * np.pi * np.outer(k1, order) / rows)
    turn = np.exp(-2j * np.pi * np.outer(k1, np.arange(LANES)) / n)
    second = np.exp(-2j * np.pi * np.outer(np.arange(LANES), np.arange(LANES)) / LANES)
    back = np.conj(second)
    last = np.conj(first).T / n
    w1 = np.concatenate([first.real, first.imag], 0)
    w3 = np.block([[second.real, second.imag], [-second.imag, second.real]])
    w4 = np.block([[back.real, back.imag], [-back.imag, back.real]])
    w6 = np.concatenate([last.real, -last.imag], 1)
    tw = np.stack([turn.real, turn.imag])
    return tuple(x.astype(np.float32) for x in (w1, w3, w4, w6, tw))


def dot(a, b):
    return jnp.dot(a, b, preferred_element_type=f32)


def kernel(
    blocks, proj, weight, filt, gain, w1, w3, w4, w6, tw, out,
    proj_v, filt_v, weight_v, gain_s, w1_v, w3_v, w4_v, w6_v, tw_v,
    halo, taps_v, query_v, spread, msg, inbox, opened, result, reply_v, back, back_f,
    load_sem, const_sem, ready, halo_send, halo_recv, send_sem, recv_sem, send2_sem, recv2_sem,
):
    chans = proj.shape[1]
    pieces = proj.shape[2] // LANES
    rows = blocks * pieces
    me = lax.axis_index("seq")
    group, place = me // (2 * GROUP), lax.rem(me, 2 * GROUP)
    holder = place < GROUP
    mine = group * GROUP + lax.rem(place, GROUP)
    groups = blocks // (2 * GROUP)

    def home(ch):
        return (ch // GROUP) * (2 * GROUP) + lax.rem(ch, GROUP)

    def tile(r):
        return slice(LANES * r, LANES * (r + 1))

    loads = [
        pltpu.make_async_copy(src, dst, load_sem.at[i])
        for i, (src, dst) in enumerate([(filt, filt_v), (proj, proj_v), (weight, weight_v), (gain, gain_s)])
    ]
    for load in loads:
        load.start()
    consts = [
        pltpu.make_async_copy(src, dst, const_sem.at[i])
        for i, (src, dst) in enumerate([(w1, w1_v), (w3, w3_v), (w4, w4_v), (w6, w6_v), (tw, tw_v)])
    ]

    barrier = pltpu.get_barrier_semaphore()

    @pl.when(holder)
    def _():
        def greet(i, carry):
            pl.semaphore_signal(
                barrier, inc=1, device_id={"seq": lax.rem(me + i, blocks)}, device_id_type=MESH
            )
            return carry

        lax.fori_loop(1, blocks, greet, 0)

    @pl.when(jnp.logical_and(place >= GROUP, place < 2 * GROUP - 1))
    def _():
        pl.semaphore_signal(barrier, inc=1, device_id={"seq": me + 1}, device_id_type=MESH)

    @pl.when(holder)
    def _():
        for const in consts:
            const.start()

    @pl.when(me == 0)
    def _():
        halo[...] = jnp.zeros_like(halo)

    after = me + 1
    pl.semaphore_wait(barrier, jnp.where(holder, chans - 1, jnp.where(place > GROUP, chans + 1, chans)))

    @pl.when(jnp.logical_not(holder))
    def _():
        pl.semaphore_signal(ready, inc=1, device_id={"seq": me - 1}, device_id_type=MESH)

    loads[0].wait()
    for r in range(pieces):
        spread[pl.ds(2 * pieces + r, chans, stride=3 * pieces), :] = filt_v[:, tile(r)].astype(f32)
    loads[1].wait()
    for j in range(2):
        for r in range(pieces):
            spread[pl.ds(j * pieces + r, chans, stride=3 * pieces), :] = proj_v[1 + j, :, tile(r)].astype(f32)
    msg[...] = spread[...].reshape(chans, 3, pieces, LANES).astype(bf16)

    def send(i, carry):
        ch = lax.rem(mine + i, chans)
        pltpu.make_async_remote_copy(
            src_ref=msg.at[ch],
            dst_ref=inbox.at[me],
            send_sem=send_sem,
            recv_sem=recv_sem,
            device_id={"seq": home(ch)},
            device_id_type=MESH,
        ).start()
        return carry

    @pl.when(jnp.logical_not(holder))
    def _():
        send(0, 0)

    lax.fori_loop(1, chans, send, 0)
    edge = pltpu.make_async_remote_copy(
        src_ref=proj_v.at[0, :, pl.ds((pieces - 1) * LANES, LANES)],
        dst_ref=halo,
        send_sem=halo_send,
        recv_sem=halo_recv,
        device_id={"seq": jnp.minimum(after, blocks - 1)},
        device_id_type=MESH,
    )

    @pl.when(jnp.logical_and(place >= GROUP - 1, place < 2 * GROUP - 1))
    def _():
        pl.semaphore_wait(ready, 1)

    @pl.when(after < blocks)
    def _():
        edge.start()

    loads[2].wait()
    for j in range(3):
        taps_v[3 * j : 3 * j + 3, :chans] = weight_v[j]
    taps_t = taps_v[...].T[:chans]
    lane = lax.broadcasted_iota(jnp.int32, (blocks, LANES), 1)

    def short(now, before, taps):
        one = pltpu.roll(jnp.where(lane[: now.shape[0]] >= LANES - 1, before, now), 1, 1)
        two = pltpu.roll(jnp.where(lane[: now.shape[0]] >= LANES - 2, before, now), 2, 1)
        total = taps[0] * two
        total = total + taps[1] * one
        total = total + taps[2] * now
        return total.astype(bf16).astype(f32)

    for r in reversed(range(pieces)):
        if r == 0:

            @pl.when(me > 0)
            def _():
                edge.wait_recv()

        now = proj_v[0, :, tile(r)].astype(f32)
        before = (halo[...] if r == 0 else proj_v[0, :, tile(r - 1)]).astype(f32)
        query_v[:, tile(r)] = short(now, before, [taps_t[:, i : i + 1] for i in range(3)])

    loads[3].wait()

    @pl.when(holder)
    def _():
        inbox[me] = msg[mine]
        for const in consts:
            const.wait()
        others = inbox.at[pl.ds(0, blocks - 1)]
        pltpu.make_async_copy(others, others, recv_sem).wait()
        opened[...] = inbox[...].astype(f32).reshape(blocks * 3 * pieces, LANES)
        part = [
            [opened[pl.ds(j * pieces + r, blocks, stride=3 * pieces), :] for r in range(pieces)]
            for j in range(3)
        ]
        chan_lane = lax.broadcasted_iota(jnp.int32, weight_v.shape[1:], 1)
        row = lax.broadcasted_iota(jnp.int32, (blocks, LANES), 0)
        conv = []
        for j in range(2):
            taps = jnp.sum(jnp.where(chan_lane == mine, weight_v[1 + j], 0.0), axis=1, keepdims=True)
            taps = [taps[i : i + 1, :] for i in range(3)]
            before = jnp.where(row == 0, 0.0, pltpu.roll(part[j][pieces - 1], 1, 0))
            done = []
            for r in range(pieces):
                done.append(short(part[j][r], before, taps))
                before = part[j][r]
            conv.append(jnp.concatenate(done, 0))
        mixed = (conv[0] * conv[1]).astype(bf16)
        both = jnp.concatenate([mixed, jnp.concatenate(part[2], 0).astype(bf16)], 1)
        step = dot(w1_v[...].astype(bf16), both)
        tr, ti = tw_v[0], tw_v[1]
        turned = []
        for half in (tile(0), tile(1)):
            re, im = step[:rows, half], step[rows:, half]
            turned.append(jnp.concatenate([re * tr - im * ti, re * ti + im * tr], 1).astype(bf16))
        spec = dot(jnp.concatenate(turned, 0), w3_v[...].astype(bf16))
        xr, xi = spec[:rows, :LANES], spec[:rows, LANES:]
        hr, hi = spec[rows:, :LANES], spec[rows:, LANES:]
        prod = jnp.concatenate([xr * hr - xi * hi, xr * hi + xi * hr], 1).astype(bf16)
        inv = dot(prod, w4_v[...].astype(bf16))
        re, im = inv[:, :LANES], inv[:, LANES:]
        untwist = jnp.concatenate([re * tr + im * ti, im * tr - re * ti], 0).astype(bf16)
        long_out = dot(w6_v[...].astype(bf16), untwist) + gain_s[mine] * mixed.astype(f32)
        for r in range(pieces):
            result[pl.ds(r, blocks, stride=pieces), :] = long_out[r * blocks : (r + 1) * blocks]
        reply_v[...] = result[...].reshape(blocks, pieces, LANES).astype(bf16)
        back[mine] = reply_v[me]

        def reply(i, carry):
            a = lax.rem(i + group, groups) * (2 * GROUP) + i // groups

            @pl.when(a != me)
            def _():
                pltpu.make_async_remote_copy(
                    src_ref=reply_v.at[a],
                    dst_ref=back.at[mine],
                    send_sem=send2_sem,
                    recv_sem=recv2_sem,
                    device_id={"seq": a},
                    device_id_type=MESH,
                ).start()

            return carry

        lax.fori_loop(0, blocks, reply, 0)
        others = back.at[pl.ds(0, chans - 1)]
        pltpu.make_async_copy(others, others, recv2_sem).wait()

    @pl.when(jnp.logical_not(holder))
    def _():
        pltpu.make_async_copy(back, back, recv2_sem).wait()

    back_f[...] = back[...].astype(f32).reshape(chans * pieces, LANES)
    for r in range(pieces):
        long_out = back_f[pl.ds(r, chans, stride=pieces), :]
        out[:, tile(r)] = (query_v[:, tile(r)] * long_out).astype(bf16)

    @pl.when(after < blocks)
    def _():
        edge.wait_send()

    @pl.when(holder)
    def _():
        sent = msg.at[pl.ds(0, chans - 1)]
        pltpu.make_async_copy(sent, sent, send_sem).wait()
        sent = reply_v.at[pl.ds(0, blocks - 1)]
        pltpu.make_async_copy(sent, sent, send2_sem).wait()

    @pl.when(jnp.logical_not(holder))
    def _():
        pltpu.make_async_copy(msg, msg, send_sem).wait()


def shards(blocks, projections, short_weight, long_filter, skip_gain):
    _, chans, tokens = projections.shape
    pieces = tokens // LANES
    rows = blocks * pieces
    consts = [jnp.asarray(x) for x in tables(blocks, pieces)]
    weight = jnp.transpose(short_weight, (0, 2, 1))
    dma = pltpu.SemaphoreType.DMA
    scratch = [
        pltpu.VMEM(projections.shape, bf16),
        pltpu.VMEM(long_filter.shape, bf16),
        pltpu.VMEM(weight.shape, f32),
        pltpu.SMEM(skip_gain.shape, f32),
        *[pltpu.VMEM(x.shape, x.dtype) for x in consts],
        pltpu.VMEM((chans, LANES), bf16),
        pltpu.VMEM((16, LANES), f32),
        pltpu.VMEM((chans, tokens), f32),
        pltpu.VMEM((chans * 3 * pieces, LANES), f32),
        pltpu.VMEM((chans, 3, pieces, LANES), bf16),
        pltpu.VMEM((blocks, 3, pieces, LANES), bf16),
        pltpu.VMEM((blocks * 3 * pieces, LANES), f32),
        pltpu.VMEM((rows, LANES), f32),
        pltpu.VMEM((blocks, pieces, LANES), bf16),
        pltpu.VMEM((chans, pieces, LANES), bf16),
        pltpu.VMEM((chans * pieces, LANES), f32),
        dma((4,)), dma((5,)), pltpu.SemaphoreType.REGULAR, dma, dma, dma, dma, dma, dma,
    ]
    return pl.pallas_call(
        functools.partial(kernel, blocks),
        out_shape=pltpu.VMEM((chans, tokens), bf16),
        in_specs=[pl.BlockSpec(memory_space=pl.ANY)] * 9,
        out_specs=pl.BlockSpec(memory_space=pltpu.VMEM),
        scratch_shapes=scratch,
        compiler_params=pltpu.CompilerParams(
            collective_id=0, has_side_effects=True, vmem_limit_bytes=56 * 1024 * 1024
        ),
        cost_estimate=pl.CostEstimate(flops=200_000_000, bytes_accessed=2_000_000, transcendentals=0),
        name="hyena",
    )(projections, weight, long_filter, skip_gain, *consts)


def solution(mesh):
    in_specs = (P(None, "chan", "seq"), P(None, "chan", None), P("chan", "seq"), P("chan"))
    out_specs = P("chan", "seq")
    body = functools.partial(shards, mesh.shape["seq"])
    return jax.shard_map(body, mesh=mesh, in_specs=in_specs, out_specs=out_specs, check_vma=False)
```

```python
import functools

import jax
import jax.numpy as jnp
import numpy as np
from jax import lax
from jax.experimental import pallas as pl
from jax.experimental.pallas import tpu as pltpu
from jax.sharding import PartitionSpec as P

MESH = pl.DeviceIdType.MESH
LANES = 128
ROW = 16
FIRST, STEP, COUNT = 1, 1, 2
f32 = jnp.float32
bf16 = jnp.bfloat16


def tables(blocks, pieces):
    rows = blocks * pieces
    n = rows * LANES
    order = (np.arange(blocks)[None, :] * pieces + np.arange(pieces)[:, None]).reshape(-1)
    k1 = np.arange(rows) + 0.25
    first = np.exp(-2j * np.pi * np.outer(k1, order) / rows)
    turn = np.exp(-2j * np.pi * np.outer(k1, np.arange(LANES)) / n)
    second = np.exp(-2j * np.pi * np.outer(np.arange(LANES), np.arange(LANES)) / LANES)
    back = np.conj(second)
    last = np.conj(first).T / n
    w1 = np.concatenate([first.real, first.imag], 0)
    w3 = np.block([[second.real, second.imag], [-second.imag, second.real]])
    w4 = np.block([[back.real, back.imag], [-back.imag, back.real]])
    w6 = np.concatenate([last.real, -last.imag], 1)
    tw = np.stack([turn.real, turn.imag])
    return tuple(x.astype(np.float32) for x in (w1, w3, w4, w6, tw))


def dot(a, b):
    return jnp.dot(a, b, preferred_element_type=f32)


def kernel(
    blocks, proj, weight, filt, gain, w1, w3, w4, w6, tw, out,
    proj_v, filt_v, weight_v, gain_s, w1_v, w3_v, w4_v, w6_v, tw_v,
    halo, taps_v, query_v, filt_s, mix_s, filt_m, mix_m, edge_m, filt_in, mix_in, edge_in, filt_o, mix_o, edge_o, spec_h,
    result, reply_v, back, back_f,
    load_sem, const_sem, ready, halo_send, halo_recv, filt_send, filt_recv, mix_send, mix_recv, edge_send, edge_recv, send2_sem, recv2_sem,
):
    chans = proj.shape[1]
    pieces = proj.shape[2] // LANES
    rows = blocks * pieces
    me = lax.axis_index("seq")
    groups = blocks // ROW
    homes = groups * 2 * COUNT
    each = chans // homes
    group, place = me // ROW, lax.rem(me, ROW)

    def holds(seq):
        chip = lax.rem(seq, ROW) // 2 - FIRST
        return (chip >= 0) & (chip < STEP * COUNT) & (lax.rem(chip + STEP * ROW, STEP) == 0)

    def home(h):
        slot = lax.rem(h, 2 * COUNT)
        return (h // (2 * COUNT)) * ROW + 2 * (FIRST + STEP * (slot // 2)) + lax.rem(slot, 2)

    holder = holds(me)
    slot = 2 * ((place // 2 - FIRST) // STEP) + lax.rem(place, 2)
    mine = group * (2 * COUNT) + jnp.where(holder, slot, lax.rem(place, 2 * COUNT))

    def tile(r):
        return slice(LANES * r, LANES * (r + 1))

    loads = [
        pltpu.make_async_copy(src, dst, load_sem.at[i])
        for i, (src, dst) in enumerate([(weight, weight_v), (filt, filt_v), (proj, proj_v), (gain, gain_s)])
    ]
    for load in loads:
        load.start()
    consts = [
        pltpu.make_async_copy(src, dst, const_sem.at[i])
        for i, (src, dst) in enumerate([(w1, w1_v), (w3, w3_v), (w4, w4_v), (w6, w6_v), (tw, tw_v)])
    ]

    barrier = pltpu.get_barrier_semaphore()

    @pl.when(holder)
    def _():
        def greet(i, carry):
            a = lax.rem(i + group, groups) * ROW + i // groups

            @pl.when(a != me)
            def _():
                pl.semaphore_signal(barrier, inc=1, device_id={"seq": a}, device_id_type=MESH)

            return carry

        lax.fori_loop(0, blocks, greet, 0)

    after = me + 1
    bare = jnp.logical_not(holder)
    next_bare = (after < blocks) & jnp.logical_not(holds(after))
    last_bare = (me > 0) & jnp.logical_not(holds(me - 1))
    row_start, row_end = place == 0, place == ROW - 1

    @pl.when(bare & next_bare & jnp.logical_not(row_end))
    def _():
        pl.semaphore_signal(barrier, inc=1, device_id={"seq": after}, device_id_type=MESH)

    @pl.when(bare & row_start & (me > 0))
    def _():
        pl.semaphore_signal(barrier, inc=1, device_id={"seq": me - 1}, device_id_type=MESH)

    @pl.when(holder)
    def _():
        for const in consts:
            const.start()

    @pl.when(me == 0)
    def _():
        halo[...] = jnp.zeros_like(halo)

    greeted = [bare & last_bare & jnp.logical_not(row_start), next_bare & row_end]
    pl.semaphore_wait(barrier, homes - holder.astype(jnp.int32) + sum(x.astype(jnp.int32) for x in greeted))

    @pl.when(bare & jnp.logical_not(row_start))
    def _():
        pl.semaphore_signal(ready, inc=1, device_id={"seq": me - 1}, device_id_type=MESH)

    def far_first(i):
        return lax.rem(group + jnp.where(i == 0, 2, jnp.where(i == groups - 1, 0, 2 * i - 1)), groups)

    def send(src, each, dst, send_sem, recv_sem):
        def one(i, carry):
            slot = lax.rem(i, 2 * COUNT)
            slot = jnp.where(place >= ROW * 3 // 4, 2 * COUNT - 1 - slot, slot)
            h = far_first(i // (2 * COUNT)) * (2 * COUNT) + slot

            @pl.when(home(h) != me)
            def _():
                pltpu.make_async_remote_copy(
                    src_ref=src.at[pl.ds(h * each, each)],
                    dst_ref=dst.at[pl.ds(me * each, each)],
                    send_sem=send_sem,
                    recv_sem=recv_sem,
                    device_id={"seq": home(h)},
                    device_id_type=MESH,
                ).start()

            return carry

        lax.fori_loop(0, homes, one, 0)

    lane = lax.broadcasted_iota(jnp.int32, (blocks, LANES), 1)

    def short(now, before, taps):
        one = pltpu.roll(jnp.where(lane[: now.shape[0]] >= LANES - 1, before, now), 1, 1)
        two = pltpu.roll(jnp.where(lane[: now.shape[0]] >= LANES - 2, before, now), 2, 1)
        total = taps[0] * two
        total = total + taps[1] * one
        total = total + taps[2] * now
        return total.astype(bf16).astype(f32)

    loads[0].wait()
    for j in range(3):
        taps_v[3 * j : 3 * j + 3, :chans] = weight_v[j]
    taps_t = taps_v[...].T[:chans]
    taps = [[taps_t[:, 3 * j + i : 3 * j + i + 1] for i in range(3)] for j in range(3)]

    loads[1].wait()
    for r in range(pieces):
        filt_s[pl.ds(r, chans, stride=pieces), :] = filt_v[:, tile(r)].astype(f32)
    filt_m[...] = filt_s[...].reshape(chans, pieces, LANES).astype(bf16)
    send(filt_m, each, filt_in, filt_send, filt_recv)

    loads[2].wait()
    here = lane[:chans]
    ends = []
    for j in (1, 2):
        head, tail = proj_v[j, :, tile(0)].astype(f32), proj_v[j, :, tile(pieces - 1)].astype(f32)
        ends.append(jnp.where(here < LANES // 2, head, tail))
    ends = jnp.where((here >= 6) & (here < 10), pltpu.roll(ends[1], 8, 1), ends[0])
    edge_m[...] = ends.reshape(homes, each, LANES).astype(bf16)
    send(edge_m, 1, edge_in, edge_send, edge_recv)

    for r in range(pieces):
        conv = []
        for j in (1, 2):
            now = proj_v[j, :, tile(r)].astype(f32)
            before = proj_v[j, :, tile(max(r - 1, 0))].astype(f32)
            conv.append(short(now, before, taps[j]))
        mix_s[pl.ds(r, chans, stride=pieces), :] = conv[0] * conv[1]
    mix_m[...] = mix_s[...].reshape(chans, pieces, LANES).astype(bf16)
    send(mix_m, each, mix_in, mix_send, mix_recv)

    edge = pltpu.make_async_remote_copy(
        src_ref=proj_v.at[0, :, pl.ds((pieces - 1) * LANES, LANES)],
        dst_ref=halo,
        send_sem=halo_send,
        recv_sem=halo_recv,
        device_id={"seq": jnp.minimum(after, blocks - 1)},
        device_id_type=MESH,
    )

    @pl.when(next_bare & jnp.logical_not(row_end))
    def _():
        pl.semaphore_wait(ready, 1)

    @pl.when(after < blocks)
    def _():
        edge.start()

    for r in reversed(range(pieces)):
        if r == 0:

            @pl.when(me > 0)
            def _():
                edge.wait_recv()

        now = proj_v[0, :, tile(r)].astype(f32)
        before = (halo[...] if r == 0 else proj_v[0, :, tile(r - 1)]).astype(f32)
        query_v[:, tile(r)] = short(now, before, taps[0])

    loads[3].wait()

    @pl.when(holder)
    def _():
        for const in consts:
            const.wait()
        tr, ti = tw_v[0], tw_v[1]

        def forward(signals):
            step = dot(w1_v[...].astype(bf16), jnp.concatenate(signals, 1))
            turned = []
            for e in range(each):
                re, im = step[:rows, tile(e)], step[rows:, tile(e)]
                turned.append(jnp.concatenate([re * tr - im * ti, re * ti + im * tr], 1).astype(bf16))
            return dot(jnp.concatenate(turned, 0), w3_v[...].astype(bf16))

        def arrived(dst, each, sem):
            others = dst.at[pl.ds(0, (blocks - 1) * each)]
            pltpu.make_async_copy(others, others, sem).wait()

        for src, dst in ((filt_m, filt_in), (mix_m, mix_in)):
            dst[pl.ds(me * each, each)] = src[pl.ds(mine * each, each)]
        edge_in[me] = edge_m[mine]
        arrived(filt_in, each, filt_recv)
        filt_o[...] = filt_in[...].astype(f32).reshape(blocks * each * pieces, LANES)

        def rows_of(opened, e):
            return [opened[pl.ds(e * pieces + r, blocks, stride=each * pieces), :] for r in range(pieces)]

        spec_h[...] = forward([jnp.concatenate(rows_of(filt_o, e), 0).astype(bf16) for e in range(each)])
        arrived(edge_in, 1, edge_recv)
        edge_o[...] = edge_in[...].astype(f32).reshape(blocks * each, LANES)
        chan_lane = lax.broadcasted_iota(jnp.int32, weight_v.shape[1:], 1)
        row = lax.broadcasted_iota(jnp.int32, (blocks, LANES), 0)
        heads = []
        for e in range(each):
            ends = edge_o[pl.ds(e, blocks, stride=each), :]
            conv = []
            for j in (1, 2):
                now = ends if j == 1 else pltpu.roll(ends, LANES - 8, 1)
                before = jnp.where(row == 0, 0.0, pltpu.roll(now, 1, 0))
                held = jnp.sum(
                    jnp.where(chan_lane == mine * each + e, weight_v[j], 0.0), axis=1, keepdims=True
                )
                conv.append(short(now, before, [held[i : i + 1, :] for i in range(3)]))
            heads.append((conv[0] * conv[1]).astype(bf16).astype(f32))
        arrived(mix_in, each, mix_recv)
        mix_o[...] = mix_in[...].astype(f32).reshape(blocks * each * pieces, LANES)
        mixes = []
        for e in range(each):
            part = rows_of(mix_o, e)
            part[0] = jnp.where(lane < 2, heads[e], part[0])
            mixes.append(jnp.concatenate(part, 0).astype(bf16))
        spec = forward(mixes)
        prods = []
        for e in range(each):
            x, h = spec[e * rows : (e + 1) * rows], spec_h[e * rows : (e + 1) * rows]
            xr, xi, hr, hi = x[:, :LANES], x[:, LANES:], h[:, :LANES], h[:, LANES:]
            prods.append(jnp.concatenate([xr * hr - xi * hi, xr * hi + xi * hr], 1).astype(bf16))
        inv = dot(jnp.concatenate(prods, 0), w4_v[...].astype(bf16))
        untwist = []
        for e in range(each):
            part = inv[e * rows : (e + 1) * rows]
            re, im = part[:, :LANES], part[:, LANES:]
            untwist.append(jnp.concatenate([re * tr + im * ti, im * tr - re * ti], 0).astype(bf16))
        long_out = dot(w6_v[...].astype(bf16), jnp.concatenate(untwist, 1))
        for e in range(each):
            total = long_out[:, tile(e)] + gain_s[mine * each + e] * mixes[e].astype(f32)
            for r in range(pieces):
                result[pl.ds(e * pieces + r, blocks, stride=each * pieces), :] = total[
                    r * blocks : (r + 1) * blocks
                ]
        reply_v[...] = result[...].reshape(blocks, each, pieces, LANES).astype(bf16)
        back[pl.ds(mine * each, each)] = reply_v[me]

        def reply(i, carry):
            a = far_first(lax.rem(i, groups)) * ROW + i // groups

            @pl.when(a != me)
            def _():
                pltpu.make_async_remote_copy(
                    src_ref=reply_v.at[a],
                    dst_ref=back.at[pl.ds(mine * each, each)],
                    send_sem=send2_sem,
                    recv_sem=recv2_sem,
                    device_id={"seq": a},
                    device_id_type=MESH,
                ).start()

            return carry

        lax.fori_loop(0, blocks, reply, 0)
        others = back.at[pl.ds(0, chans - each)]
        pltpu.make_async_copy(others, others, recv2_sem).wait()

    @pl.when(jnp.logical_not(holder))
    def _():
        pltpu.make_async_copy(back, back, recv2_sem).wait()

    back_f[...] = back[...].astype(f32).reshape(chans * pieces, LANES)
    for r in range(pieces):
        long_out = back_f[pl.ds(r, chans, stride=pieces), :]
        out[:, tile(r)] = (query_v[:, tile(r)] * long_out).astype(bf16)

    @pl.when(after < blocks)
    def _():
        edge.wait_send()

    sends = ((filt_m, each, filt_send), (mix_m, each, mix_send), (edge_m, 1, edge_send))

    @pl.when(holder)
    def _():
        for src, step, sem in sends:
            sent = src.at[pl.ds(0, (homes - 1) * step)]
            pltpu.make_async_copy(sent, sent, sem).wait()
        sent = reply_v.at[pl.ds(0, blocks - 1)]
        pltpu.make_async_copy(sent, sent, send2_sem).wait()

    @pl.when(jnp.logical_not(holder))
    def _():
        for src, _, sem in sends:
            pltpu.make_async_copy(src, src, sem).wait()


def shards(blocks, projections, short_weight, long_filter, skip_gain):
    _, chans, tokens = projections.shape
    pieces = tokens // LANES
    each = chans // (blocks // ROW * 2 * COUNT)
    rows = blocks * pieces
    consts = [jnp.asarray(x) for x in tables(blocks, pieces)]
    weight = jnp.transpose(short_weight, (0, 2, 1))
    dma = pltpu.SemaphoreType.DMA
    scratch = [
        pltpu.VMEM(projections.shape, bf16),
        pltpu.VMEM(long_filter.shape, bf16),
        pltpu.VMEM(weight.shape, f32),
        pltpu.SMEM(skip_gain.shape, f32),
        *[pltpu.VMEM(x.shape, x.dtype) for x in consts],
        pltpu.VMEM((chans, LANES), bf16),
        pltpu.VMEM((16, LANES), f32),
        pltpu.VMEM((chans, tokens), f32),
        pltpu.VMEM((chans * pieces, LANES), f32),
        pltpu.VMEM((chans * pieces, LANES), f32),
        pltpu.VMEM((chans, pieces, LANES), bf16),
        pltpu.VMEM((chans, pieces, LANES), bf16),
        pltpu.VMEM((chans // each, each, LANES), bf16),
        pltpu.VMEM((blocks * each, pieces, LANES), bf16),
        pltpu.VMEM((blocks * each, pieces, LANES), bf16),
        pltpu.VMEM((blocks, each, LANES), bf16),
        pltpu.VMEM((blocks * each * pieces, LANES), f32),
        pltpu.VMEM((blocks * each * pieces, LANES), f32),
        pltpu.VMEM((blocks * each, LANES), f32),
        pltpu.VMEM((each * rows, 2 * LANES), f32),
        pltpu.VMEM((rows * each, LANES), f32),
        pltpu.VMEM((blocks, each, pieces, LANES), bf16),
        pltpu.VMEM((chans, pieces, LANES), bf16),
        pltpu.VMEM((chans * pieces, LANES), f32),
        dma((4,)), dma((5,)), pltpu.SemaphoreType.REGULAR, *[dma] * 10,
    ]
    return pl.pallas_call(
        functools.partial(kernel, blocks),
        out_shape=pltpu.VMEM((chans, tokens), bf16),
        in_specs=[pl.BlockSpec(memory_space=pl.ANY)] * 9,
        out_specs=pl.BlockSpec(memory_space=pltpu.VMEM),
        scratch_shapes=scratch,
        compiler_params=pltpu.CompilerParams(
            collective_id=0, has_side_effects=True, vmem_limit_bytes=56 * 1024 * 1024
        ),
        cost_estimate=pl.CostEstimate(flops=200_000_000, bytes_accessed=2_000_000, transcendentals=0),
        name="hyena",
    )(projections, weight, long_filter, skip_gain, *consts)


def solution(mesh):
    in_specs = (P(None, "chan", "seq"), P(None, "chan", None), P("chan", "seq"), P("chan"))
    out_specs = P("chan", "seq")
    body = functools.partial(shards, mesh.shape["seq"])
    return jax.shard_map(body, mesh=mesh, in_specs=in_specs, out_specs=out_specs, check_vma=False)
```

```python
import functools

import jax
import jax.numpy as jnp
import numpy as np
from jax import lax
from jax.experimental import pallas as pl
from jax.experimental.pallas import tpu as pltpu
from jax.sharding import PartitionSpec as P

MESH = pl.DeviceIdType.MESH
LANES = 128
ROW = 16
FIRST, COUNT = 1, 1
GREET = (5, 6, 4, 7, 3, 0, 2, 1)
f32 = jnp.float32
bf16 = jnp.bfloat16


def tables(blocks, pieces):
    rows = blocks * pieces
    n = rows * LANES
    order = (np.arange(blocks)[None, :] * pieces + np.arange(pieces)[:, None]).reshape(-1)
    k1 = np.arange(rows) + 0.25
    first = np.exp(-2j * np.pi * np.outer(k1, order) / rows)
    turn = np.exp(-2j * np.pi * np.outer(k1, np.arange(LANES)) / n)
    second = np.exp(-2j * np.pi * np.outer(np.arange(LANES), np.arange(LANES)) / LANES)
    back = np.conj(second)
    last = np.conj(first).T / n
    w1 = np.concatenate([first.real, first.imag], 0)
    w3 = np.block([[second.real, second.imag], [-second.imag, second.real]])
    w4 = np.block([[back.real, back.imag], [-back.imag, back.real]])
    w6 = np.concatenate([last.real, -last.imag], 1)
    tw = np.stack([turn.real, turn.imag])
    return tuple(x.astype(np.float32) for x in (w1, w3, w4, w6, tw))


def dot(a, b):
    return jnp.dot(a, b, preferred_element_type=f32)


def kernel(
    blocks, proj, weight, filt, gain, w1, w3, w4, w6, tw, out,
    proj_v, filt_v, weight_v, gain_s, w1_v, w3_v, w4_v, w6_v, tw_v,
    halo, taps_v, query_v, filt_s, mix_s, filt_m, mix_m, edge_m, filt_in, mix_in, edge_in, filt_o, mix_o, edge_o, spec_h,
    w1_b, w3_b, w4_b, w6_b,
    result, reply_v, back, back_f,
    load_sem, const_sem, ready, halo_send, halo_recv, filt_send, filt_recv, mix_send, mix_recv, edge_send, edge_recv, send2_sem, recv2_sem,
):
    chans = proj.shape[1]
    pieces = proj.shape[2] // LANES
    rows = blocks * pieces
    me = lax.axis_index("seq")
    groups = blocks // ROW
    homes = groups * 2 * COUNT
    each = chans // homes
    group, place = me // ROW, lax.rem(me, ROW)

    far_first = [lax.rem(group + step, groups) for step in (2, 1, 3, 0)[-groups:]]

    def holds(seq):
        chip = lax.rem(seq, ROW) // 2 - FIRST
        return (chip >= 0) & (chip < COUNT)

    holder = holds(me)
    mine = group * (2 * COUNT) + jnp.where(holder, place - 2 * FIRST, 0)

    def tile(r):
        return slice(LANES * r, LANES * (r + 1))

    loads = [
        pltpu.make_async_copy(src, dst, load_sem.at[i])
        for i, (src, dst) in enumerate([(weight, weight_v), (filt, filt_v), (proj, proj_v), (gain, gain_s)])
    ]
    for load in loads:
        load.start()
    consts = [
        pltpu.make_async_copy(src, dst, const_sem.at[i])
        for i, (src, dst) in enumerate([(w1, w1_v), (w3, w3_v), (w4, w4_v), (w6, w6_v), (tw, tw_v)])
    ]

    barrier = pltpu.get_barrier_semaphore()

    @pl.when(holder)
    def _():
        for place_to in [2 * z + c for z in GREET for c in (0, 1)]:
            for g in far_first:
                a = g * ROW + place_to

                @pl.when(a != me)
                def _():
                    pl.semaphore_signal(barrier, inc=1, device_id={"seq": a}, device_id_type=MESH)

    after = me + 1
    bare = jnp.logical_not(holder)
    next_bare = (after < blocks) & jnp.logical_not(holds(after))
    last_bare = (me > 0) & jnp.logical_not(holds(me - 1))
    row_start, row_end = place == 0, place == ROW - 1

    @pl.when(bare & next_bare & jnp.logical_not(row_end))
    def _():
        pl.semaphore_signal(barrier, inc=1, device_id={"seq": after}, device_id_type=MESH)

    @pl.when(bare & row_start & (me > 0))
    def _():
        pl.semaphore_signal(barrier, inc=1, device_id={"seq": me - 1}, device_id_type=MESH)

    @pl.when(holder)
    def _():
        for const in consts:
            const.start()

    @pl.when(me == 0)
    def _():
        halo[...] = jnp.zeros_like(halo)

    greeted = [bare & last_bare & jnp.logical_not(row_start), next_bare & row_end]
    pl.semaphore_wait(barrier, homes - holder.astype(jnp.int32) + sum(x.astype(jnp.int32) for x in greeted))

    @pl.when(bare & jnp.logical_not(row_start))
    def _():
        pl.semaphore_signal(ready, inc=1, device_id={"seq": me - 1}, device_id_type=MESH)

    half = groups // 2
    turn_of = jnp.where((place < ROW // 2) | (group < half - 1), 0, 1)
    spans = [[], []]
    for g in range(groups):
        spans[0].append(g * ROW)
        spans[0 if g < half - 1 else 1].append(g * ROW + ROW // 2)

    def send(src, each, dst, send_sem, recv_sem):
        for g in far_first:
            for k in range(2 * COUNT):
                slot = jnp.where(place >= ROW * 3 // 4, 2 * COUNT - 1 - k, k)
                h, to = g * (2 * COUNT) + slot, g * ROW + 2 * FIRST + slot

                @pl.when(to != me)
                def _():
                    pltpu.make_async_remote_copy(
                        src_ref=src.at[pl.ds(h * each, each)],
                        dst_ref=dst.at[pl.ds(me * each, each)],
                        send_sem=send_sem,
                        recv_sem=recv_sem.at[turn_of],
                        device_id={"seq": to},
                        device_id_type=MESH,
                    ).start()

    lane = lax.broadcasted_iota(jnp.int32, (blocks, LANES), 1)

    def short(now, before, taps):
        one = pltpu.roll(jnp.where(lane[: now.shape[0]] >= LANES - 1, before, now), 1, 1)
        two = pltpu.roll(jnp.where(lane[: now.shape[0]] >= LANES - 2, before, now), 2, 1)
        total = taps[0] * two
        total = total + taps[1] * one
        total = total + taps[2] * now
        return total.astype(bf16).astype(f32)

    loads[0].wait()
    for j in range(3):
        taps_v[3 * j : 3 * j + 3, :chans] = weight_v[j]
    taps_t = taps_v[...].T[:chans]
    taps = [[taps_t[:, 3 * j + i : 3 * j + i + 1] for i in range(3)] for j in range(3)]

    loads[1].wait()
    for r in range(pieces):
        filt_s[pl.ds(r, chans, stride=pieces), :] = filt_v[:, tile(r)].astype(f32)
    filt_m[...] = filt_s[...].reshape(chans, pieces, LANES).astype(bf16)
    send(filt_m, each, filt_in, filt_send, filt_recv)

    loads[2].wait()
    here = lane[:chans]
    ends = []
    for j in (1, 2):
        head, tail = proj_v[j, :, tile(0)].astype(f32), proj_v[j, :, tile(pieces - 1)].astype(f32)
        ends.append(jnp.where(here < LANES // 2, head, tail))
    ends = jnp.where((here >= 6) & (here < 10), pltpu.roll(ends[1], 8, 1), ends[0])
    edge_m[...] = ends.reshape(homes, each, LANES).astype(bf16)
    send(edge_m, 1, edge_in, edge_send, edge_recv)

    for r in range(pieces):
        conv = []
        for j in (1, 2):
            now = proj_v[j, :, tile(r)].astype(f32)
            before = proj_v[j, :, tile(max(r - 1, 0))].astype(f32)
            conv.append(short(now, before, taps[j]))
        mix_s[pl.ds(r, chans, stride=pieces), :] = conv[0] * conv[1]
    mix_m[...] = mix_s[...].reshape(chans, pieces, LANES).astype(bf16)
    send(mix_m, each, mix_in, mix_send, mix_recv)

    edge = pltpu.make_async_remote_copy(
        src_ref=proj_v.at[0, :, pl.ds((pieces - 1) * LANES, LANES)],
        dst_ref=halo,
        send_sem=halo_send,
        recv_sem=halo_recv,
        device_id={"seq": jnp.minimum(after, blocks - 1)},
        device_id_type=MESH,
    )

    @pl.when(next_bare & jnp.logical_not(row_end))
    def _():
        pl.semaphore_wait(ready, 1)

    @pl.when(after < blocks)
    def _():
        edge.start()

    for r in reversed(range(pieces)):
        if r == 0:

            @pl.when(me > 0)
            def _():
                edge.wait_recv()

        now = proj_v[0, :, tile(r)].astype(f32)
        before = (halo[...] if r == 0 else proj_v[0, :, tile(r - 1)]).astype(f32)
        query_v[:, tile(r)] = short(now, before, taps[0])

    loads[3].wait()

    @pl.when(holder)
    def _():
        for const in consts:
            const.wait()
        for src, dst in zip((w1_v, w3_v, w4_v, w6_v), (w1_b, w3_b, w4_b, w6_b)):
            dst[...] = src[...].astype(bf16)
        tr, ti = tw_v[0], tw_v[1]
        for opened in (filt_o, mix_o, edge_o):
            opened[...] = jnp.zeros_like(opened)
        for src, dst in ((filt_m, filt_in), (mix_m, mix_in)):
            dst[pl.ds(me * each, each)] = src[pl.ds(mine * each, each)]
        edge_in[me] = edge_m[mine]
        chan_lane = lax.broadcasted_iota(jnp.int32, weight_v.shape[1:], 1)
        row = lax.broadcasted_iota(jnp.int32, (blocks, LANES), 0)
        held = []
        for e in range(each):
            here = chan_lane == mine * each + e
            rows_j = [jnp.sum(jnp.where(here, weight_v[j], 0.0), axis=1, keepdims=True) for j in (1, 2)]
            held.append([[x[i : i + 1, :] for i in range(3)] for x in rows_j])

        def forward(signals):
            step = dot(w1_b[...], jnp.concatenate(signals, 1))
            turned = []
            for e in range(each):
                re, im = step[:rows, tile(e)], step[rows:, tile(e)]
                turned.append(jnp.concatenate([re * tr - im * ti, re * ti + im * tr], 1).astype(bf16))
            return dot(jnp.concatenate(turned, 0), w3_b[...])

        def take(turn, src, step, lines, dst, sem):
            count = len(spans[turn]) * (ROW // 2) - (1 if turn == 0 else 0)
            others = src.at[pl.ds(0, count * step)]
            pltpu.make_async_copy(others, others, sem.at[turn]).wait()
            for a in spans[turn]:
                b = a + ROW // 2
                fresh = src[a * step : b * step].astype(f32)
                dst[a * lines : b * lines, :] = fresh.reshape((b - a) * lines, LANES)

        def rows_of(opened, e):
            return [opened[pl.ds(e * pieces + r, blocks, stride=each * pieces), :] for r in range(pieces)]

        for turn in range(2):
            take(turn, filt_in, each, each * pieces, filt_o, filt_recv)
            spec_h[...] = forward([jnp.concatenate(rows_of(filt_o, e), 0).astype(bf16) for e in range(each)])
            take(turn, edge_in, 1, each, edge_o, edge_recv)
            heads = []
            for e in range(each):
                ends = edge_o[pl.ds(e, blocks, stride=each), :]
                conv = []
                for now, taps in zip((ends, pltpu.roll(ends, LANES - 8, 1)), held[e]):
                    conv.append(short(now, jnp.where(row == 0, 0.0, pltpu.roll(now, 1, 0)), taps))
                heads.append((conv[0] * conv[1]).astype(bf16).astype(f32))
            take(turn, mix_in, each, each * pieces, mix_o, mix_recv)
            mixes = []
            for e in range(each):
                part = rows_of(mix_o, e)
                part[0] = jnp.where(lane < 2, heads[e], part[0])
                mixes.append(jnp.concatenate(part, 0).astype(bf16))
            spec = forward(mixes)
            prods = []
            for e in range(each):
                x, h = spec[e * rows : (e + 1) * rows], spec_h[e * rows : (e + 1) * rows]
                xr, xi, hr, hi = x[:, :LANES], x[:, LANES:], h[:, :LANES], h[:, LANES:]
                prods.append(jnp.concatenate([xr * hr - xi * hi, xr * hi + xi * hr], 1).astype(bf16))
            inv = dot(jnp.concatenate(prods, 0), w4_b[...])
            untwist = []
            for e in range(each):
                part = inv[e * rows : (e + 1) * rows]
                re, im = part[:, :LANES], part[:, LANES:]
                untwist.append(jnp.concatenate([re * tr + im * ti, im * tr - re * ti], 0).astype(bf16))
            long_out = dot(w6_b[...], jnp.concatenate(untwist, 1))
            for e in range(each):
                total = long_out[:, tile(e)] + gain_s[mine * each + e] * mixes[e].astype(f32)
                for r in range(pieces):
                    result[pl.ds(e * pieces + r, blocks, stride=each * pieces), :] = total[
                        r * blocks : (r + 1) * blocks
                    ]
            reply_v[turn] = result[...].reshape(blocks, each, pieces, LANES).astype(bf16)

            @pl.when((group < half) if turn == 0 else (group >= half))
            def _():
                back[pl.ds(mine * each, each)] = reply_v[turn, me]

            early = [(p, g) for p in range(ROW // 2) for g in range(groups) if (g < half) == (turn == 0)]
            late = [(p, g) for p in range(ROW // 2, ROW) for g in range(groups) if turn == 1]
            for place_to, g in early + late:
                a = g * ROW + place_to

                @pl.when(me != a)
                def _():
                    pltpu.make_async_remote_copy(
                        src_ref=reply_v.at[turn, a],
                        dst_ref=back.at[pl.ds(mine * each, each)],
                        send_sem=send2_sem,
                        recv_sem=recv2_sem,
                        device_id={"seq": a},
                        device_id_type=MESH,
                    ).start()

        others = back.at[pl.ds(0, chans - each)]
        pltpu.make_async_copy(others, others, recv2_sem).wait()

    @pl.when(jnp.logical_not(holder))
    def _():
        pltpu.make_async_copy(back, back, recv2_sem).wait()

    back_f[...] = back[...].astype(f32).reshape(chans * pieces, LANES)
    for r in range(pieces):
        long_out = back_f[pl.ds(r, chans, stride=pieces), :]
        out[:, tile(r)] = (query_v[:, tile(r)] * long_out).astype(bf16)

    @pl.when(after < blocks)
    def _():
        edge.wait_send()

    sends = ((filt_m, each, filt_send), (mix_m, each, mix_send), (edge_m, 1, edge_send))

    @pl.when(holder)
    def _():
        for src, step, sem in sends:
            sent = src.at[pl.ds(0, (homes - 1) * step)]
            pltpu.make_async_copy(sent, sent, sem).wait()
        sent = reply_v.at[0, pl.ds(0, blocks - 1)]
        pltpu.make_async_copy(sent, sent, send2_sem).wait()

    @pl.when(jnp.logical_not(holder))
    def _():
        for src, _, sem in sends:
            pltpu.make_async_copy(src, src, sem).wait()


def shards(blocks, projections, short_weight, long_filter, skip_gain):
    _, chans, tokens = projections.shape
    pieces = tokens // LANES
    each = chans // (blocks // ROW * 2 * COUNT)
    rows = blocks * pieces
    consts = [jnp.asarray(x) for x in tables(blocks, pieces)]
    weight = jnp.transpose(short_weight, (0, 2, 1))
    dma = pltpu.SemaphoreType.DMA
    scratch = [
        pltpu.VMEM(projections.shape, bf16),
        pltpu.VMEM(long_filter.shape, bf16),
        pltpu.VMEM(weight.shape, f32),
        pltpu.SMEM(skip_gain.shape, f32),
        *[pltpu.VMEM(x.shape, x.dtype) for x in consts],
        pltpu.VMEM((chans, LANES), bf16),
        pltpu.VMEM((16, LANES), f32),
        pltpu.VMEM((chans, tokens), f32),
        pltpu.VMEM((chans * pieces, LANES), f32),
        pltpu.VMEM((chans * pieces, LANES), f32),
        pltpu.VMEM((chans, pieces, LANES), bf16),
        pltpu.VMEM((chans, pieces, LANES), bf16),
        pltpu.VMEM((chans // each, each, LANES), bf16),
        pltpu.VMEM((blocks * each, pieces, LANES), bf16),
        pltpu.VMEM((blocks * each, pieces, LANES), bf16),
        pltpu.VMEM((blocks, each, LANES), bf16),
        pltpu.VMEM((blocks * each * pieces, LANES), f32),
        pltpu.VMEM((blocks * each * pieces, LANES), f32),
        pltpu.VMEM((blocks * each, LANES), f32),
        pltpu.VMEM((each * rows, 2 * LANES), f32),
        *[pltpu.VMEM(x.shape, bf16) for x in consts[:4]],
        pltpu.VMEM((rows * each, LANES), f32),
        pltpu.VMEM((2, blocks, each, pieces, LANES), bf16),
        pltpu.VMEM((chans, pieces, LANES), bf16),
        pltpu.VMEM((chans * pieces, LANES), f32),
        dma((4,)), dma((5,)), pltpu.SemaphoreType.REGULAR, dma, dma, *[dma, dma((2,))] * 3, dma, dma,
    ]
    return pl.pallas_call(
        functools.partial(kernel, blocks),
        out_shape=pltpu.VMEM((chans, tokens), bf16),
        in_specs=[pl.BlockSpec(memory_space=pl.ANY)] * 9,
        out_specs=pl.BlockSpec(memory_space=pltpu.VMEM),
        scratch_shapes=scratch,
        compiler_params=pltpu.CompilerParams(
            collective_id=0, has_side_effects=True, vmem_limit_bytes=56 * 1024 * 1024
        ),
        cost_estimate=pl.CostEstimate(flops=200_000_000, bytes_accessed=2_000_000, transcendentals=0),
        name="hyena",
    )(projections, weight, long_filter, skip_gain, *consts)


def solution(mesh):
    in_specs = (P(None, "chan", "seq"), P(None, "chan", None), P("chan", "seq"), P("chan"))
    out_specs = P("chan", "seq")
    body = functools.partial(shards, mesh.shape["seq"])
    return jax.shard_map(body, mesh=mesh, in_specs=in_specs, out_specs=out_specs, check_vma=False)
```

```python
import functools

import jax
import jax.numpy as jnp
import numpy as np
from jax import lax
from jax.experimental import pallas as pl
from jax.experimental.pallas import tpu as pltpu
from jax.sharding import PartitionSpec as P

MESH = pl.DeviceIdType.MESH
LANES = 128
ROW = 16
FIRST, COUNT = 1, 1
GREET = (5, 6, 4, 7, 3, 0, 2, 1)
f32 = jnp.float32
bf16 = jnp.bfloat16


def tables(blocks, pieces):
    rows = blocks * pieces
    n = rows * LANES
    k1 = np.arange(rows) + 0.25
    first = np.exp(-2j * np.pi * np.outer(k1, np.arange(rows)) / rows)
    turn = np.exp(-2j * np.pi * np.outer(k1, np.arange(LANES)) / n)
    second = np.exp(-2j * np.pi * np.outer(np.arange(LANES), np.arange(LANES)) / LANES)
    back = np.conj(second)
    last = np.conj(first).T / n
    w1 = np.concatenate([first.real, first.imag], 0)
    w3 = np.block([[second.real, second.imag], [-second.imag, second.real]])
    w4 = np.block([[back.real, back.imag], [-back.imag, back.real]])
    w6 = np.concatenate([last.real, -last.imag], 1)
    tw = np.stack([turn.real, turn.imag])
    return tuple(x.astype(np.float32) for x in (w1, w6, tw, w3, w4))


def dot(a, b):
    return jnp.dot(a, b, preferred_element_type=f32)


def kernel(
    blocks, proj, weight, filt, gain, w1, w6, tw, w3, w4, w1_half, w6_half, tw_half, out,
    proj_v, filt_v, weight_v, gain_s, w1_v, w6_v, tw_v, w3_v, w4_v, w1_half_v, w6_half_v, tw_half_v,
    w1_b, w6_b, w3_b, w4_b, w1_half_b, w6_half_b,
    halo, taps_v, query_v, filt_s, mix_s, filt_m, mix_m, edge_m, filt_in, mix_in, edge_in, edge_o, heads, spec_h,
    reply_v, back, back_f,
    load_sem, const_sem, ready, halo_send, halo_recv, filt_send, filt_recv, mix_send, mix_recv, edge_send, edge_recv,
    send2_sem, recv2_sem,
):
    chans = proj.shape[1]
    pieces = proj.shape[2] // LANES
    me = lax.axis_index("seq")
    groups = blocks // ROW
    homes = groups * 2 * COUNT
    each = chans // homes
    group, place = me // ROW, lax.rem(me, ROW)

    far_first = [lax.rem(group + step, groups) for step in (2, 1, 3, 0)[-groups:]]

    def holds(seq):
        chip = lax.rem(seq, ROW) // 2 - FIRST
        return (chip >= 0) & (chip < COUNT)

    holder = holds(me)
    mine = group * (2 * COUNT) + jnp.where(holder, place - 2 * FIRST, 0)

    def tile(r):
        return slice(LANES * r, LANES * (r + 1))

    loads = [
        pltpu.make_async_copy(src, dst, load_sem.at[i])
        for i, (src, dst) in enumerate([(weight, weight_v), (filt, filt_v), (proj, proj_v), (gain, gain_s)])
    ]
    for load in loads:
        load.start()
    consts = [
        pltpu.make_async_copy(src, dst, const_sem.at[i])
        for i, (src, dst) in enumerate(
            [(w1, w1_v), (w6, w6_v), (tw, tw_v), (w3, w3_v), (w4, w4_v)]
            + [(w1_half, w1_half_v), (w6_half, w6_half_v), (tw_half, tw_half_v)]
        )
    ]

    barrier = pltpu.get_barrier_semaphore()

    @pl.when(holder)
    def _():
        for place_to in [2 * z + c for z in GREET for c in (0, 1)]:
            for g in far_first:
                a = g * ROW + place_to

                @pl.when(a != me)
                def _():
                    pl.semaphore_signal(barrier, inc=1, device_id={"seq": a}, device_id_type=MESH)

    after = me + 1
    bare = jnp.logical_not(holder)
    next_bare = (after < blocks) & jnp.logical_not(holds(after))
    last_bare = (me > 0) & jnp.logical_not(holds(me - 1))
    row_start, row_end = place == 0, place == ROW - 1

    @pl.when(bare & next_bare & jnp.logical_not(row_end))
    def _():
        pl.semaphore_signal(barrier, inc=1, device_id={"seq": after}, device_id_type=MESH)

    @pl.when(bare & row_start & (me > 0))
    def _():
        pl.semaphore_signal(barrier, inc=1, device_id={"seq": me - 1}, device_id_type=MESH)

    @pl.when(holder)
    def _():
        for const in consts:
            const.start()

    @pl.when(me == 0)
    def _():
        halo[...] = jnp.zeros_like(halo)

    greeted = [bare & last_bare & jnp.logical_not(row_start), next_bare & row_end]
    pl.semaphore_wait(barrier, homes - holder.astype(jnp.int32) + sum(x.astype(jnp.int32) for x in greeted))

    @pl.when(bare & jnp.logical_not(row_start))
    def _():
        pl.semaphore_signal(ready, inc=1, device_id={"seq": me - 1}, device_id_type=MESH)

    half = groups // 2
    ahead = half * ROW - ROW // 2
    counts = (ahead, blocks - ahead)
    turn_of = jnp.where(me < ahead, 0, 1)

    def send(src, dst, send_sem, recv_sem):
        step = src.shape[0] // homes

        for g in far_first:
            for k in range(2 * COUNT):
                slot = jnp.where(place >= ROW * 3 // 4, 2 * COUNT - 1 - k, k)
                h, to = g * (2 * COUNT) + slot, g * ROW + 2 * FIRST + slot
                part = src.at[pl.ds(h * step, step)]

                @pl.when(to != me)
                def _():
                    pltpu.make_async_remote_copy(
                        src_ref=part,
                        dst_ref=dst.at[:, me],
                        send_sem=send_sem,
                        recv_sem=recv_sem.at[turn_of],
                        device_id={"seq": to},
                        device_id_type=MESH,
                    ).start()

        @pl.when(holder)
        def _():
            pltpu.make_async_copy(src.at[pl.ds(mine * step, step)], dst.at[:, me], recv_sem.at[turn_of]).start()

    lane = lax.broadcasted_iota(jnp.int32, (blocks, LANES), 1)

    def short(now, before, taps):
        one = pltpu.roll(jnp.where(lane[: now.shape[0]] >= LANES - 1, before, now), 1, 1)
        two = pltpu.roll(jnp.where(lane[: now.shape[0]] >= LANES - 2, before, now), 2, 1)
        total = taps[0] * two
        total = total + taps[1] * one
        total = total + taps[2] * now
        return total.astype(bf16).astype(f32)

    loads[0].wait()
    for j in range(3):
        taps_v[3 * j : 3 * j + 3, :chans] = weight_v[j]
    taps_t = taps_v[...].T[:chans]
    taps = [[taps_t[:, 3 * j + i : 3 * j + i + 1] for i in range(3)] for j in range(3)]

    loads[1].wait()
    for r in range(pieces):
        filt_s[pl.ds(r, chans, stride=pieces), :] = filt_v[:, tile(r)].astype(f32)
    filt_m[...] = filt_s[...].reshape(chans, pieces, LANES).astype(bf16)
    send(filt_m, filt_in, filt_send, filt_recv)

    loads[2].wait()
    here = lane[:chans]
    ends = []
    for j in (1, 2):
        head, tail = proj_v[j, :, tile(0)].astype(f32), proj_v[j, :, tile(pieces - 1)].astype(f32)
        ends.append(jnp.where(here < LANES // 2, head, tail))
    ends = jnp.where((here >= 6) & (here < 10), pltpu.roll(ends[1], 8, 1), ends[0])
    edge_m[...] = ends.reshape(edge_m.shape).astype(bf16)
    send(edge_m, edge_in, edge_send, edge_recv)

    for r in range(pieces):
        conv = []
        for j in (1, 2):
            now = proj_v[j, :, tile(r)].astype(f32)
            before = proj_v[j, :, tile(max(r - 1, 0))].astype(f32)
            conv.append(short(now, before, taps[j]))
        mix_s[pl.ds(r, chans, stride=pieces), :] = conv[0] * conv[1]
    mix_m[...] = mix_s[...].reshape(chans, pieces, LANES).astype(bf16)
    send(mix_m, mix_in, mix_send, mix_recv)

    edge = pltpu.make_async_remote_copy(
        src_ref=proj_v.at[0, :, pl.ds((pieces - 1) * LANES, LANES)],
        dst_ref=halo,
        send_sem=halo_send,
        recv_sem=halo_recv,
        device_id={"seq": jnp.minimum(after, blocks - 1)},
        device_id_type=MESH,
    )

    @pl.when(next_bare & jnp.logical_not(row_end))
    def _():
        pl.semaphore_wait(ready, 1)

    @pl.when(after < blocks)
    def _():
        edge.start()

    for r in reversed(range(pieces)):
        if r == 0:

            @pl.when(me > 0)
            def _():
                edge.wait_recv()

        now = proj_v[0, :, tile(r)].astype(f32)
        before = (halo[...] if r == 0 else proj_v[0, :, tile(r - 1)]).astype(f32)
        query_v[:, tile(r)] = short(now, before, taps[0])

    loads[3].wait()

    @pl.when(holder)
    def _():
        for const in consts:
            const.wait()
        for src, dst in (
            (w1_v, w1_b), (w6_v, w6_b), (w3_v, w3_b), (w4_v, w4_b), (w1_half_v, w1_half_b), (w6_half_v, w6_half_b)
        ):
            dst[...] = src[...].astype(bf16)
        edge_o[...] = jnp.zeros_like(edge_o)
        chan_lane = lax.broadcasted_iota(jnp.int32, weight_v.shape[1:], 1)
        held = []
        for e in range(each):
            here = chan_lane == mine * each + e
            rows_j = [jnp.sum(jnp.where(here, weight_v[j], 0.0), axis=1, keepdims=True) for j in (1, 2)]
            held.append([[x[i : i + 1, :] for i in range(3)] for x in rows_j])

        def arrived(turn, dst, sem):
            some = dst.at[:, pl.ds(0, counts[turn])]
            pltpu.make_async_copy(some, some, sem.at[turn]).wait()

        for turn in range(2):
            count = (half * ROW, blocks)[turn]
            known = (ahead, blocks)[turn]
            rows = count * pieces
            first, last, turns = ((w1_half_b, w6_half_b, tw_half_v), (w1_b, w6_b, tw_v))[turn]
            tr, ti = turns[0], turns[1]
            row = lax.broadcasted_iota(jnp.int32, (rows, LANES), 0)
            column = lax.broadcasted_iota(jnp.int32, (rows, LANES), 1)

            def signal(src, e):
                got = src[e, :known].astype(f32).reshape(known * pieces, LANES)
                if known < count:
                    got = jnp.concatenate([got, jnp.zeros((rows - known * pieces, LANES), f32)], 0)
                return got

            def forward(signals):
                step = dot(first[...], jnp.concatenate(signals, 1))
                turned = []
                for e in range(each):
                    re, im = step[:rows, tile(e)], step[rows:, tile(e)]
                    turned.append(jnp.concatenate([re * tr - im * ti, re * ti + im * tr], 1).astype(bf16))
                return dot(jnp.concatenate(turned, 0), w3_b[...])

            arrived(turn, filt_in, filt_recv)
            spec_h[: each * rows] = forward([signal(filt_in, e).astype(bf16) for e in range(each)])
            arrived(turn, edge_in, edge_recv)
            fresh = edge_in[0, :known, 0].astype(f32)
            edge_o[: known * each, :] = fresh.reshape(known * each, LANES)
            for e in range(each):
                ends = edge_o[pl.ds(e, count, stride=each), :]
                conv = []
                for now, taps in zip((ends, pltpu.roll(ends, LANES - 8, 1)), held[e]):
                    conv.append(short(now, jnp.where(row[:count] == 0, 0.0, pltpu.roll(now, 1, 0)), taps))
                heads[e, pl.ds(0, count, stride=pieces), :] = conv[0] * conv[1]
            arrived(turn, mix_in, mix_recv)
            start = (column < 2) & (lax.rem(row, pieces) == 0)
            mixes = [jnp.where(start, heads[e, :rows], signal(mix_in, e)).astype(bf16) for e in range(each)]
            spec = forward(mixes)
            prods = []
            for e in range(each):
                x, h = spec[e * rows : (e + 1) * rows], spec_h[e * rows : (e + 1) * rows]
                xr, xi, hr, hi = x[:, :LANES], x[:, LANES:], h[:, :LANES], h[:, LANES:]
                prods.append(jnp.concatenate([xr * hr - xi * hi, xr * hi + xi * hr], 1).astype(bf16))
            inv = dot(jnp.concatenate(prods, 0), w4_b[...])
            untwist = []
            for e in range(each):
                part = inv[e * rows : (e + 1) * rows]
                re, im = part[:, :LANES], part[:, LANES:]
                untwist.append(jnp.concatenate([re * tr + im * ti, im * tr - re * ti], 0).astype(bf16))
            long_out = dot(last[...], jnp.concatenate(untwist, 1))
            for e in range(each):
                total = long_out[:, tile(e)] + gain_s[mine * each + e] * mixes[e].astype(f32)
                reply_v[turn, e, :count] = total.reshape(count, pieces, LANES).astype(bf16)

            @pl.when((group < half) if turn == 0 else (group >= half))
            def _():
                back[pl.ds(mine * each, each)] = reply_v[turn, :, me]

            early = [(p, g) for p in range(ROW // 2) for g in range(groups) if (g < half) == (turn == 0)]
            late = [(p, g) for p in range(ROW // 2, ROW) for g in range(groups) if turn == 1]
            for place_to, g in early + late:
                a = g * ROW + place_to

                @pl.when(me != a)
                def _():
                    pltpu.make_async_remote_copy(
                        src_ref=reply_v.at[turn, :, a],
                        dst_ref=back.at[pl.ds(mine * each, each)],
                        send_sem=send2_sem,
                        recv_sem=recv2_sem,
                        device_id={"seq": a},
                        device_id_type=MESH,
                    ).start()

        others = back.at[pl.ds(0, chans - each)]
        pltpu.make_async_copy(others, others, recv2_sem).wait()

    @pl.when(jnp.logical_not(holder))
    def _():
        pltpu.make_async_copy(back, back, recv2_sem).wait()

    back_f[...] = back[...].astype(f32).reshape(chans * pieces, LANES)
    for r in range(pieces):
        long_out = back_f[pl.ds(r, chans, stride=pieces), :]
        out[:, tile(r)] = (query_v[:, tile(r)] * long_out).astype(bf16)

    @pl.when(after < blocks)
    def _():
        edge.wait_send()

    sends = ((filt_m, filt_send), (mix_m, mix_send), (edge_m, edge_send))

    @pl.when(holder)
    def _():
        for src, sem in sends:
            sent = src.at[pl.ds(0, src.shape[0] // homes * (homes - 1))]
            pltpu.make_async_copy(sent, sent, sem).wait()
        sent = reply_v.at[0, :, pl.ds(0, blocks - 1)]
        pltpu.make_async_copy(sent, sent, send2_sem).wait()

    @pl.when(jnp.logical_not(holder))
    def _():
        for src, sem in sends:
            pltpu.make_async_copy(src, src, sem).wait()


def shards(blocks, projections, short_weight, long_filter, skip_gain):
    _, chans, tokens = projections.shape
    pieces = tokens // LANES
    each = chans // (blocks // ROW * 2 * COUNT)
    rows = blocks * pieces
    consts = [jnp.asarray(x) for x in tables(blocks, pieces) + tables(blocks // 2, pieces)[:3]]
    weight = jnp.transpose(short_weight, (0, 2, 1))
    dma = pltpu.SemaphoreType.DMA
    scratch = [
        pltpu.VMEM(projections.shape, bf16),
        pltpu.VMEM(long_filter.shape, bf16),
        pltpu.VMEM(weight.shape, f32),
        pltpu.SMEM(skip_gain.shape, f32),
        *[pltpu.VMEM(x.shape, x.dtype) for x in consts],
        *[pltpu.VMEM(consts[i].shape, bf16) for i in (0, 1, 3, 4, 5, 6)],
        pltpu.VMEM((chans, LANES), bf16),
        pltpu.VMEM((16, LANES), f32),
        pltpu.VMEM((chans, tokens), f32),
        pltpu.VMEM((chans * pieces, LANES), f32),
        pltpu.VMEM((chans * pieces, LANES), f32),
        pltpu.VMEM((chans, pieces, LANES), bf16),
        pltpu.VMEM((chans, pieces, LANES), bf16),
        pltpu.VMEM((chans // each, 1, each, LANES), bf16),
        pltpu.VMEM((each, blocks, pieces, LANES), bf16),
        pltpu.VMEM((each, blocks, pieces, LANES), bf16),
        pltpu.VMEM((1, blocks, 1, each, LANES), bf16),
        pltpu.VMEM((blocks * each, LANES), f32),
        pltpu.VMEM((each, rows, LANES), f32),
        pltpu.VMEM((each * rows, 2 * LANES), f32),
        pltpu.VMEM((2, each, blocks, pieces, LANES), bf16),
        pltpu.VMEM((chans, pieces, LANES), bf16),
        pltpu.VMEM((chans * pieces, LANES), f32),
        dma((4,)), dma((8,)), pltpu.SemaphoreType.REGULAR, dma, dma, *[dma, dma((2,))] * 3, dma, dma,
    ]
    return pl.pallas_call(
        functools.partial(kernel, blocks),
        out_shape=pltpu.VMEM((chans, tokens), bf16),
        in_specs=[pl.BlockSpec(memory_space=pl.ANY)] * 12,
        out_specs=pl.BlockSpec(memory_space=pltpu.VMEM),
        scratch_shapes=scratch,
        compiler_params=pltpu.CompilerParams(
            collective_id=0, has_side_effects=True, vmem_limit_bytes=56 * 1024 * 1024
        ),
        cost_estimate=pl.CostEstimate(flops=200_000_000, bytes_accessed=2_000_000, transcendentals=0),
        name="hyena",
    )(projections, weight, long_filter, skip_gain, *consts)


def solution(mesh):
    in_specs = (P(None, "chan", "seq"), P(None, "chan", None), P("chan", "seq"), P("chan"))
    out_specs = P("chan", "seq")
    body = functools.partial(shards, mesh.shape["seq"])
    return jax.shard_map(body, mesh=mesh, in_specs=in_specs, out_specs=out_specs, check_vma=False)
```

```python
import functools

import jax
import jax.numpy as jnp
import numpy as np
from jax import lax
from jax.experimental import pallas as pl
from jax.experimental.pallas import tpu as pltpu
from jax.sharding import PartitionSpec as P

MESH = pl.DeviceIdType.MESH
LANES = 128
ROW = 16
FIRST, COUNT = 1, 1
GREET = (0, 2, 3, 1, 4, 5, 6, 7)
f32 = jnp.float32
bf16 = jnp.bfloat16


def tables(blocks, pieces):
    rows = blocks * pieces
    n = rows * LANES
    k1 = np.arange(rows) + 0.25
    first = np.exp(-2j * np.pi * np.outer(k1, np.arange(rows)) / rows)
    turn = np.exp(-2j * np.pi * np.outer(k1, np.arange(LANES)) / n)
    second = np.exp(-2j * np.pi * np.outer(np.arange(LANES), np.arange(LANES)) / LANES)
    back = np.conj(second)
    last = np.conj(first).T / n
    w1 = np.concatenate([first.real, first.imag], 0)
    w3 = np.block([[second.real, second.imag], [-second.imag, second.real]])
    w4 = np.block([[back.real, back.imag], [-back.imag, back.real]])
    w6 = np.concatenate([last.real, -last.imag], 1)
    tw = np.stack([turn.real, turn.imag])
    return tuple(x.astype(np.float32) for x in (w1, w6, tw, w3, w4))


def dot(a, b):
    return jnp.dot(a, b, preferred_element_type=f32)


def kernel(
    blocks, proj, weight, filt, gain, w1, w6, tw, w3, w4, w1_half, w6_half, tw_half, out,
    proj_v, filt_v, weight_v, gain_s, w1_v, w6_v, tw_v, w3_v, w4_v, w1_half_v, w6_half_v, tw_half_v,
    w1_b, w6_b, w3_b, w4_b, w1_half_b, w6_half_b,
    halo, taps_v, query_v, filt_s, mix_s, filt_m, mix_m, edge_m, filt_in, mix_in, edge_in, edge_o, heads, spec_h,
    reply_v, back, back_f,
    load_sem, const_sem, ready, halo_send, halo_recv, filt_send, filt_recv, mix_send, mix_recv, edge_send, edge_recv,
    send2_sem, recv2_sem,
):
    chans = proj.shape[1]
    pieces = proj.shape[2] // LANES
    me = lax.axis_index("seq")
    groups = blocks // ROW
    homes = groups * 2 * COUNT
    each = chans // homes
    group, place = me // ROW, lax.rem(me, ROW)

    far_first = [lax.rem(group + step, groups) for step in (2, 1, 3, 0)[-groups:]]

    def holds(seq):
        chip = lax.rem(seq, ROW) // 2 - FIRST
        return (chip >= 0) & (chip < COUNT)

    holder = holds(me)
    mine = group * (2 * COUNT) + jnp.where(holder, place - 2 * FIRST, 0)

    def tile(r):
        return slice(LANES * r, LANES * (r + 1))

    loads = [
        pltpu.make_async_copy(src, dst, load_sem.at[i])
        for i, (src, dst) in enumerate(
            [(weight, weight_v), (filt, filt_v), (proj.at[1], proj_v.at[1]), (proj.at[2], proj_v.at[2])]
            + [(proj.at[0], proj_v.at[0]), (gain, gain_s)]
        )
    ]
    for load in loads:
        load.start()
    consts = [
        pltpu.make_async_copy(src, dst, const_sem.at[i])
        for i, (src, dst) in enumerate(
            [(w1, w1_v), (w6, w6_v), (tw, tw_v), (w3, w3_v), (w4, w4_v)]
            + [(w1_half, w1_half_v), (w6_half, w6_half_v), (tw_half, tw_half_v)]
        )
    ]

    barrier = pltpu.get_barrier_semaphore()

    @pl.when(holder)
    def _():
        for place_to in [2 * z + c for z in GREET for c in (0, 1)]:
            for g in far_first:
                a = g * ROW + place_to

                @pl.when(a != me)
                def _():
                    pl.semaphore_signal(barrier, inc=1, device_id={"seq": a}, device_id_type=MESH)

    after = me + 1
    bare = jnp.logical_not(holder)
    next_bare = (after < blocks) & jnp.logical_not(holds(after))
    last_bare = (me > 0) & jnp.logical_not(holds(me - 1))
    row_start, row_end = place == 0, place == ROW - 1

    @pl.when(bare & next_bare & jnp.logical_not(row_end))
    def _():
        pl.semaphore_signal(barrier, inc=1, device_id={"seq": after}, device_id_type=MESH)

    @pl.when(bare & row_start & (me > 0))
    def _():
        pl.semaphore_signal(barrier, inc=1, device_id={"seq": me - 1}, device_id_type=MESH)

    @pl.when(holder)
    def _():
        for const in consts:
            const.start()

    @pl.when(me == 0)
    def _():
        halo[...] = jnp.zeros_like(halo)

    greeted = [bare & last_bare & jnp.logical_not(row_start), next_bare & row_end]
    pl.semaphore_wait(barrier, homes - holder.astype(jnp.int32) + sum(x.astype(jnp.int32) for x in greeted))

    @pl.when(bare & jnp.logical_not(row_start))
    def _():
        pl.semaphore_signal(ready, inc=1, device_id={"seq": me - 1}, device_id_type=MESH)

    half = groups // 2
    ends_at = (ROW // 2, half * ROW - ROW // 2, blocks)
    counts = [b - a for a, b in zip((0, *ends_at), ends_at)]
    turn_of = sum((me >= b).astype(jnp.int32) for b in ends_at[:-1])
    asked = [range(1), range(1, half), range(half, groups)]

    def send(src, dst, send_sem, recv_sem):
        step = src.shape[0] // homes

        for g in far_first:
            for k in range(2 * COUNT):
                slot = jnp.where(place >= ROW * 3 // 4, 2 * COUNT - 1 - k, k)
                h, to = g * (2 * COUNT) + slot, g * ROW + 2 * FIRST + slot
                part = src.at[pl.ds(h * step, step)]

                @pl.when(to != me)
                def _():
                    pltpu.make_async_remote_copy(
                        src_ref=part,
                        dst_ref=dst.at[:, me],
                        send_sem=send_sem,
                        recv_sem=recv_sem.at[turn_of],
                        device_id={"seq": to},
                        device_id_type=MESH,
                    ).start()

        @pl.when(holder)
        def _():
            pltpu.make_async_copy(src.at[pl.ds(mine * step, step)], dst.at[:, me], recv_sem.at[turn_of]).start()

    lane = lax.broadcasted_iota(jnp.int32, (blocks, LANES), 1)

    def short(now, before, taps):
        one = pltpu.roll(jnp.where(lane[: now.shape[0]] >= LANES - 1, before, now), 1, 1)
        two = pltpu.roll(jnp.where(lane[: now.shape[0]] >= LANES - 2, before, now), 2, 1)
        total = taps[0] * two
        total = total + taps[1] * one
        total = total + taps[2] * now
        return total.astype(bf16).astype(f32)

    loads[0].wait()
    for j in range(3):
        taps_v[3 * j : 3 * j + 3, :chans] = weight_v[j]
    taps_t = taps_v[...].T[:chans]
    taps = [[taps_t[:, 3 * j + i : 3 * j + i + 1] for i in range(3)] for j in range(3)]

    loads[1].wait()
    for r in range(pieces):
        filt_s[pl.ds(r, chans, stride=pieces), :] = filt_v[:, tile(r)].astype(f32)
    filt_m[...] = filt_s[...].reshape(chans, pieces, LANES).astype(bf16)
    send(filt_m, filt_in, filt_send, filt_recv)

    loads[2].wait()
    loads[3].wait()
    here = lane[:chans]
    ends = []
    for j in (1, 2):
        head, tail = proj_v[j, :, tile(0)].astype(f32), proj_v[j, :, tile(pieces - 1)].astype(f32)
        ends.append(jnp.where(here < LANES // 2, head, tail))
    ends = jnp.where((here >= 6) & (here < 10), pltpu.roll(ends[1], 8, 1), ends[0])
    edge_m[...] = ends.reshape(edge_m.shape).astype(bf16)
    send(edge_m, edge_in, edge_send, edge_recv)

    for r in range(pieces):
        conv = []
        for j in (1, 2):
            now = proj_v[j, :, tile(r)].astype(f32)
            before = proj_v[j, :, tile(max(r - 1, 0))].astype(f32)
            conv.append(short(now, before, taps[j]))
        mix_s[pl.ds(r, chans, stride=pieces), :] = conv[0] * conv[1]
    mix_m[...] = mix_s[...].reshape(chans, pieces, LANES).astype(bf16)
    send(mix_m, mix_in, mix_send, mix_recv)

    loads[4].wait()
    edge = pltpu.make_async_remote_copy(
        src_ref=proj_v.at[0, :, pl.ds((pieces - 1) * LANES, LANES)],
        dst_ref=halo,
        send_sem=halo_send,
        recv_sem=halo_recv,
        device_id={"seq": jnp.minimum(after, blocks - 1)},
        device_id_type=MESH,
    )

    @pl.when(next_bare & jnp.logical_not(row_end))
    def _():
        pl.semaphore_wait(ready, 1)

    @pl.when(after < blocks)
    def _():
        edge.start()

    for r in reversed(range(pieces)):
        if r == 0:

            @pl.when(me > 0)
            def _():
                edge.wait_recv()

        now = proj_v[0, :, tile(r)].astype(f32)
        before = (halo[...] if r == 0 else proj_v[0, :, tile(r - 1)]).astype(f32)
        query_v[:, tile(r)] = short(now, before, taps[0])

    loads[5].wait()

    @pl.when(holder)
    def _():
        for const in consts:
            const.wait()
        for src, dst in (
            (w1_v, w1_b), (w6_v, w6_b), (w3_v, w3_b), (w4_v, w4_b), (w1_half_v, w1_half_b), (w6_half_v, w6_half_b)
        ):
            dst[...] = src[...].astype(bf16)
        edge_o[...] = jnp.zeros_like(edge_o)
        chan_lane = lax.broadcasted_iota(jnp.int32, weight_v.shape[1:], 1)
        held = []
        for e in range(each):
            here = chan_lane == mine * each + e
            rows_j = [jnp.sum(jnp.where(here, weight_v[j], 0.0), axis=1, keepdims=True) for j in (1, 2)]
            held.append([[x[i : i + 1, :] for i in range(3)] for x in rows_j])

        def arrived(turn, dst, sem):
            some = dst.at[:, pl.ds(0, counts[turn])]
            pltpu.make_async_copy(some, some, sem.at[turn]).wait()

        def answer(places):
            for turn, place_to, g in places:
                a = g * ROW + place_to

                @pl.when(me != a)
                def _():
                    pltpu.make_async_remote_copy(
                        src_ref=reply_v.at[turn, :, a],
                        dst_ref=back.at[pl.ds(mine * each, each)],
                        send_sem=send2_sem,
                        recv_sem=recv2_sem,
                        device_id={"seq": a},
                        device_id_type=MESH,
                    ).start()

        for turn, known in enumerate(ends_at):
            count = half * ROW if turn < 2 else blocks
            rows = count * pieces
            first, last, turns = (w1_half_b, w6_half_b, tw_half_v) if turn < 2 else (w1_b, w6_b, tw_v)
            tr, ti = turns[0], turns[1]
            row = lax.broadcasted_iota(jnp.int32, (rows, LANES), 0)
            column = lax.broadcasted_iota(jnp.int32, (rows, LANES), 1)

            def signal(src, e):
                got = src[e, :known].astype(f32).reshape(known * pieces, LANES)
                if known < count:
                    got = jnp.concatenate([got, jnp.zeros((rows - known * pieces, LANES), f32)], 0)
                return got

            def forward(signals):
                step = dot(first[...], jnp.concatenate(signals, 1))
                turned = []
                for e in range(each):
                    re, im = step[:rows, tile(e)], step[rows:, tile(e)]
                    turned.append(jnp.concatenate([re * tr - im * ti, re * ti + im * tr], 1).astype(bf16))
                return dot(jnp.concatenate(turned, 0), w3_b[...])

            arrived(turn, filt_in, filt_recv)
            spec_h[: each * rows] = forward([signal(filt_in, e).astype(bf16) for e in range(each)])
            arrived(turn, edge_in, edge_recv)
            fresh = edge_in[0, :known, 0].astype(f32)
            edge_o[: known * each, :] = fresh.reshape(known * each, LANES)
            for e in range(each):
                ends = edge_o[pl.ds(e, count, stride=each), :]
                conv = []
                for now, taps in zip((ends, pltpu.roll(ends, LANES - 8, 1)), held[e]):
                    conv.append(short(now, jnp.where(row[:count] == 0, 0.0, pltpu.roll(now, 1, 0)), taps))
                heads[e, pl.ds(0, count, stride=pieces), :] = conv[0] * conv[1]
            arrived(turn, mix_in, mix_recv)
            start = (column < 2) & (lax.rem(row, pieces) == 0)
            mixes = [jnp.where(start, heads[e, :rows], signal(mix_in, e)).astype(bf16) for e in range(each)]
            spec = forward(mixes)
            prods = []
            for e in range(each):
                x, h = spec[e * rows : (e + 1) * rows], spec_h[e * rows : (e + 1) * rows]
                xr, xi, hr, hi = x[:, :LANES], x[:, LANES:], h[:, :LANES], h[:, LANES:]
                prods.append(jnp.concatenate([xr * hr - xi * hi, xr * hi + xi * hr], 1).astype(bf16))
            inv = dot(jnp.concatenate(prods, 0), w4_b[...])
            untwist = []
            for e in range(each):
                part = inv[e * rows : (e + 1) * rows]
                re, im = part[:, :LANES], part[:, LANES:]
                untwist.append(jnp.concatenate([re * tr + im * ti, im * tr - re * ti], 0).astype(bf16))
            untwisted = jnp.concatenate(untwist, 1)

            def finish(firsts):
                some = [slice(a * pieces, (a + ROW // 2) * pieces) for a in firsts]
                long_out = dot(jnp.concatenate([last[x] for x in some], 0), untwisted)
                for e in range(each):
                    mixed = jnp.concatenate([mixes[e][x] for x in some], 0).astype(f32)
                    total = long_out[:, tile(e)] + gain_s[mine * each + e] * mixed
                    total = total.reshape(len(some) * (ROW // 2), pieces, LANES).astype(bf16)
                    for i, a in enumerate(firsts):
                        reply_v[turn, e, a : a + ROW // 2] = total[i * (ROW // 2) : (i + 1) * (ROW // 2)]

            near, far, late = range(ROW // 4), range(ROW // 4, ROW // 2), range(ROW // 2, ROW)
            finish([g * ROW for g in asked[turn]])
            answer([(turn, p, g) for p in near for g in asked[turn]])
            if turn == 0:
                answer([(0, p, g) for p in far for g in asked[0]])
            if turn == 2:
                answer([(t, p, g) for p in far for t in (1, 2) for g in asked[t]])
                finish([g * ROW + ROW // 2 for g in range(groups)])
                answer([(2, p, g) for p in late for g in range(groups)])

            @pl.when((group >= asked[turn].start) & (group < asked[turn].stop))
            def _():
                back[pl.ds(mine * each, each)] = reply_v[turn, :, me]

        others = back.at[pl.ds(0, chans - each)]
        pltpu.make_async_copy(others, others, recv2_sem).wait()

    @pl.when(jnp.logical_not(holder))
    def _():
        pltpu.make_async_copy(back, back, recv2_sem).wait()

    back_f[...] = back[...].astype(f32).reshape(chans * pieces, LANES)
    for r in range(pieces):
        long_out = back_f[pl.ds(r, chans, stride=pieces), :]
        out[:, tile(r)] = (query_v[:, tile(r)] * long_out).astype(bf16)

    @pl.when(after < blocks)
    def _():
        edge.wait_send()

    sends = ((filt_m, filt_send), (mix_m, mix_send), (edge_m, edge_send))

    @pl.when(holder)
    def _():
        for src, sem in sends:
            sent = src.at[pl.ds(0, src.shape[0] // homes * (homes - 1))]
            pltpu.make_async_copy(sent, sent, sem).wait()
        sent = reply_v.at[0, :, pl.ds(0, blocks - 1)]
        pltpu.make_async_copy(sent, sent, send2_sem).wait()

    @pl.when(jnp.logical_not(holder))
    def _():
        for src, sem in sends:
            pltpu.make_async_copy(src, src, sem).wait()


def shards(blocks, projections, short_weight, long_filter, skip_gain):
    _, chans, tokens = projections.shape
    pieces = tokens // LANES
    each = chans // (blocks // ROW * 2 * COUNT)
    rows = blocks * pieces
    consts = [jnp.asarray(x) for x in tables(blocks, pieces) + tables(blocks // 2, pieces)[:3]]
    weight = jnp.transpose(short_weight, (0, 2, 1))
    dma = pltpu.SemaphoreType.DMA
    scratch = [
        pltpu.VMEM(projections.shape, bf16),
        pltpu.VMEM(long_filter.shape, bf16),
        pltpu.VMEM(weight.shape, f32),
        pltpu.SMEM(skip_gain.shape, f32),
        *[pltpu.VMEM(x.shape, x.dtype) for x in consts],
        *[pltpu.VMEM(consts[i].shape, bf16) for i in (0, 1, 3, 4, 5, 6)],
        pltpu.VMEM((chans, LANES), bf16),
        pltpu.VMEM((16, LANES), f32),
        pltpu.VMEM((chans, tokens), f32),
        pltpu.VMEM((chans * pieces, LANES), f32),
        pltpu.VMEM((chans * pieces, LANES), f32),
        pltpu.VMEM((chans, pieces, LANES), bf16),
        pltpu.VMEM((chans, pieces, LANES), bf16),
        pltpu.VMEM((chans // each, 1, each, LANES), bf16),
        pltpu.VMEM((each, blocks, pieces, LANES), bf16),
        pltpu.VMEM((each, blocks, pieces, LANES), bf16),
        pltpu.VMEM((1, blocks, 1, each, LANES), bf16),
        pltpu.VMEM((blocks * each, LANES), f32),
        pltpu.VMEM((each, rows, LANES), f32),
        pltpu.VMEM((each * rows, 2 * LANES), f32),
        pltpu.VMEM((3, each, blocks, pieces, LANES), bf16),
        pltpu.VMEM((chans, pieces, LANES), bf16),
        pltpu.VMEM((chans * pieces, LANES), f32),
        dma((6,)), dma((8,)), pltpu.SemaphoreType.REGULAR, dma, dma, *[dma, dma((3,))] * 3, dma, dma,
    ]
    return pl.pallas_call(
        functools.partial(kernel, blocks),
        out_shape=pltpu.VMEM((chans, tokens), bf16),
        in_specs=[pl.BlockSpec(memory_space=pl.ANY)] * 12,
        out_specs=pl.BlockSpec(memory_space=pltpu.VMEM),
        scratch_shapes=scratch,
        compiler_params=pltpu.CompilerParams(
            collective_id=0, has_side_effects=True, vmem_limit_bytes=56 * 1024 * 1024
        ),
        cost_estimate=pl.CostEstimate(flops=200_000_000, bytes_accessed=2_000_000, transcendentals=0),
        name="hyena",
    )(projections, weight, long_filter, skip_gain, *consts)


def solution(mesh):
    in_specs = (P(None, "chan", "seq"), P(None, "chan", None), P("chan", "seq"), P("chan"))
    out_specs = P("chan", "seq")
    body = functools.partial(shards, mesh.shape["seq"])
    return jax.shard_map(body, mesh=mesh, in_specs=in_specs, out_specs=out_specs, check_vma=False)
```

```python
import functools

import jax
import jax.numpy as jnp
import numpy as np
from jax import lax
from jax.experimental import pallas as pl
from jax.experimental.pallas import tpu as pltpu
from jax.sharding import PartitionSpec as P

MESH = pl.DeviceIdType.MESH
LANES = 128
ROW = 16
FIRST, COUNT = 1, 1
GREET = (0, 2, 3, 1, 4, 5, 6, 7)
f32 = jnp.float32
bf16 = jnp.bfloat16


def tables(blocks, pieces):
    rows = blocks * pieces
    n = rows * LANES
    k1 = np.arange(rows) + 0.25
    first = np.exp(-2j * np.pi * np.outer(k1, np.arange(rows)) / rows)
    turn = np.exp(-2j * np.pi * np.outer(k1, np.arange(LANES)) / n)
    second = np.exp(-2j * np.pi * np.outer(np.arange(LANES), np.arange(LANES)) / LANES)
    back = np.conj(second)
    last = np.conj(first).T / n
    w1 = np.concatenate([first.real, first.imag], 0)
    w3 = np.block([[second.real, second.imag], [-second.imag, second.real]])
    w4 = np.block([[back.real, back.imag], [-back.imag, back.real]])
    w6 = np.concatenate([last.real, -last.imag], 1)
    tw = np.stack([turn.real, turn.imag])
    return tuple(x.astype(np.float32) for x in (w1, w6, tw, w3, w4))


def dot(a, b):
    return jnp.dot(a, b, preferred_element_type=f32)


def kernel(
    blocks, proj, weight, filt, gain, w1, w6, tw, w3, w4, w1_half, w6_half, tw_half, out,
    proj_v, filt_v, weight_v, gain_s, w1_v, w6_v, tw_v, w3_v, w4_v, w1_half_v, w6_half_v, tw_half_v,
    w1_b, w6_b, w3_b, w4_b, w1_half_b, w6_half_b,
    halo, taps_v, query_v, filt_s, mix_s, filt_m, mix_m, filt_in, mix_in, edge_o, heads, spec_h,
    reply_v, back, back_f,
    load_sem, const_sem, ready, halo_send, halo_recv, filt_send, filt_recv, mix_send, mix_recv,
    send2_sem, recv2_sem,
):
    chans = proj.shape[1]
    pieces = proj.shape[2] // LANES
    me = lax.axis_index("seq")
    groups = blocks // ROW
    homes = groups * 2 * COUNT
    each = chans // homes
    group, place = me // ROW, lax.rem(me, ROW)

    far_first = [lax.rem(group + step, groups) for step in (2, 1, 3, 0)[-groups:]]

    def holds(seq):
        chip = lax.rem(seq, ROW) // 2 - FIRST
        return (chip >= 0) & (chip < COUNT)

    holder = holds(me)
    mine = group * (2 * COUNT) + jnp.where(holder, place - 2 * FIRST, 0)

    def tile(r):
        return slice(LANES * r, LANES * (r + 1))

    loads = [
        pltpu.make_async_copy(src, dst, load_sem.at[i])
        for i, (src, dst) in enumerate(
            [(weight, weight_v), (filt, filt_v), (proj.at[1], proj_v.at[1]), (proj.at[2], proj_v.at[2])]
            + [(proj.at[0], proj_v.at[0]), (gain, gain_s)]
        )
    ]
    for load in loads:
        load.start()
    consts = [
        pltpu.make_async_copy(src, dst, const_sem.at[i])
        for i, (src, dst) in enumerate(
            [(w1, w1_v), (w6, w6_v), (tw, tw_v), (w3, w3_v), (w4, w4_v)]
            + [(w1_half, w1_half_v), (w6_half, w6_half_v), (tw_half, tw_half_v)]
        )
    ]

    barrier = pltpu.get_barrier_semaphore()

    @pl.when(holder)
    def _():
        for place_to in [2 * z + c for z in GREET for c in (0, 1)]:
            for g in far_first:
                a = g * ROW + place_to

                @pl.when(a != me)
                def _():
                    pl.semaphore_signal(barrier, inc=1, device_id={"seq": a}, device_id_type=MESH)

    after = me + 1
    bare = jnp.logical_not(holder)
    next_bare = (after < blocks) & jnp.logical_not(holds(after))
    last_bare = (me > 0) & jnp.logical_not(holds(me - 1))
    row_start, row_end = place == 0, place == ROW - 1

    @pl.when(bare & next_bare & jnp.logical_not(row_end))
    def _():
        pl.semaphore_signal(barrier, inc=1, device_id={"seq": after}, device_id_type=MESH)

    @pl.when(bare & row_start & (me > 0))
    def _():
        pl.semaphore_signal(barrier, inc=1, device_id={"seq": me - 1}, device_id_type=MESH)

    @pl.when(holder)
    def _():
        for const in consts:
            const.start()

    @pl.when(me == 0)
    def _():
        halo[...] = jnp.zeros_like(halo)

    greeted = [bare & last_bare & jnp.logical_not(row_start), next_bare & row_end]
    pl.semaphore_wait(barrier, homes - holder.astype(jnp.int32) + sum(x.astype(jnp.int32) for x in greeted))

    @pl.when(bare & jnp.logical_not(row_start))
    def _():
        pl.semaphore_signal(ready, inc=1, device_id={"seq": me - 1}, device_id_type=MESH)

    half = groups // 2
    ends_at = (ROW // 2, half * ROW - ROW // 2, blocks)
    counts = [b - a for a, b in zip((0, *ends_at), ends_at)]
    turn_of = sum((me >= b).astype(jnp.int32) for b in ends_at[:-1])
    asked = [range(1), range(1, half), range(half, groups)]

    def send(src, dst, send_sem, recv_sem):
        step = src.shape[0] // homes

        for g in far_first:
            for k in range(2 * COUNT):
                slot = jnp.where(place >= ROW * 3 // 4, 2 * COUNT - 1 - k, k)
                h, to = g * (2 * COUNT) + slot, g * ROW + 2 * FIRST + slot
                part = src.at[pl.ds(h * step, step)]

                @pl.when(to != me)
                def _():
                    pltpu.make_async_remote_copy(
                        src_ref=part,
                        dst_ref=dst.at[:, me],
                        send_sem=send_sem,
                        recv_sem=recv_sem.at[turn_of],
                        device_id={"seq": to},
                        device_id_type=MESH,
                    ).start()

        @pl.when(holder)
        def _():
            pltpu.make_async_copy(src.at[pl.ds(mine * step, step)], dst.at[:, me], recv_sem.at[turn_of]).start()

    lane = lax.broadcasted_iota(jnp.int32, (blocks, LANES), 1)

    def short(now, before, taps):
        one = pltpu.roll(jnp.where(lane[: now.shape[0]] >= LANES - 1, before, now), 1, 1)
        two = pltpu.roll(jnp.where(lane[: now.shape[0]] >= LANES - 2, before, now), 2, 1)
        total = taps[0] * two
        total = total + taps[1] * one
        total = total + taps[2] * now
        return total.astype(bf16).astype(f32)

    loads[0].wait()
    for j in range(3):
        taps_v[3 * j : 3 * j + 3, :chans] = weight_v[j]
    taps_t = taps_v[...].T[:chans]
    taps = [[taps_t[:, 3 * j + i : 3 * j + i + 1] for i in range(3)] for j in range(3)]

    loads[2].wait()
    loads[3].wait()
    here = lane[:chans]
    ends = []
    for j in (1, 2):
        head, tail = proj_v[j, :, tile(0)].astype(f32), proj_v[j, :, tile(pieces - 1)].astype(f32)
        ends.append(jnp.where(here < LANES // 2, head, tail))
    ends = jnp.where((here >= 6) & (here < 10), pltpu.roll(ends[1], 8, 1), ends[0])

    loads[1].wait()
    for r in range(pieces):
        filt_s[pl.ds(r, chans, stride=pieces), :] = filt_v[:, tile(r)].astype(f32)
    parts = [filt_s[...].reshape(homes, each, pieces, LANES), ends.reshape(homes, 1, each, LANES)]
    filt_m[...] = jnp.concatenate(parts, 1).reshape(filt_m.shape).astype(bf16)
    send(filt_m, filt_in, filt_send, filt_recv)


    for r in range(pieces):
        conv = []
        for j in (1, 2):
            now = proj_v[j, :, tile(r)].astype(f32)
            before = proj_v[j, :, tile(max(r - 1, 0))].astype(f32)
            conv.append(short(now, before, taps[j]))
        mix_s[pl.ds(r, chans, stride=pieces), :] = conv[0] * conv[1]
    mix_m[...] = mix_s[...].reshape(chans, pieces, LANES).astype(bf16)
    send(mix_m, mix_in, mix_send, mix_recv)

    loads[4].wait()
    edge = pltpu.make_async_remote_copy(
        src_ref=proj_v.at[0, :, pl.ds((pieces - 1) * LANES, LANES)],
        dst_ref=halo,
        send_sem=halo_send,
        recv_sem=halo_recv,
        device_id={"seq": jnp.minimum(after, blocks - 1)},
        device_id_type=MESH,
    )

    @pl.when(next_bare & jnp.logical_not(row_end))
    def _():
        pl.semaphore_wait(ready, 1)

    @pl.when(after < blocks)
    def _():
        edge.start()

    for r in reversed(range(pieces)):
        if r == 0:

            @pl.when(me > 0)
            def _():
                edge.wait_recv()

        now = proj_v[0, :, tile(r)].astype(f32)
        before = (halo[...] if r == 0 else proj_v[0, :, tile(r - 1)]).astype(f32)
        query_v[:, tile(r)] = short(now, before, taps[0])

    loads[5].wait()

    @pl.when(holder)
    def _():
        for const in consts:
            const.wait()
        for src, dst in (
            (w1_v, w1_b), (w6_v, w6_b), (w3_v, w3_b), (w4_v, w4_b), (w1_half_v, w1_half_b), (w6_half_v, w6_half_b)
        ):
            dst[...] = src[...].astype(bf16)
        edge_o[...] = jnp.zeros_like(edge_o)
        chan_lane = lax.broadcasted_iota(jnp.int32, weight_v.shape[1:], 1)
        held = []
        for e in range(each):
            here = chan_lane == mine * each + e
            rows_j = [jnp.sum(jnp.where(here, weight_v[j], 0.0), axis=1, keepdims=True) for j in (1, 2)]
            held.append([[x[i : i + 1, :] for i in range(3)] for x in rows_j])

        def arrived(turn, dst, sem):
            some = dst.at[:, pl.ds(0, counts[turn])]
            pltpu.make_async_copy(some, some, sem.at[turn]).wait()

        def answer(places):
            for turn, place_to, g in places:
                a = g * ROW + place_to

                @pl.when(me != a)
                def _():
                    pltpu.make_async_remote_copy(
                        src_ref=reply_v.at[turn, :, a],
                        dst_ref=back.at[pl.ds(mine * each, each)],
                        send_sem=send2_sem,
                        recv_sem=recv2_sem,
                        device_id={"seq": a},
                        device_id_type=MESH,
                    ).start()

        for turn, known in enumerate(ends_at):
            count = half * ROW if turn < 2 else blocks
            rows = count * pieces
            first, last, turns = (w1_half_b, w6_half_b, tw_half_v) if turn < 2 else (w1_b, w6_b, tw_v)
            tr, ti = turns[0], turns[1]
            row = lax.broadcasted_iota(jnp.int32, (rows, LANES), 0)
            column = lax.broadcasted_iota(jnp.int32, (rows, LANES), 1)

            def signal(src, e):
                got = src[e, :known].astype(f32).reshape(known * pieces, LANES)
                if known < count:
                    got = jnp.concatenate([got, jnp.zeros((rows - known * pieces, LANES), f32)], 0)
                return got

            def forward(signals):
                step = dot(first[...], jnp.concatenate(signals, 1))
                turned = []
                for e in range(each):
                    re, im = step[:rows, tile(e)], step[rows:, tile(e)]
                    turned.append(jnp.concatenate([re * tr - im * ti, re * ti + im * tr], 1).astype(bf16))
                return dot(jnp.concatenate(turned, 0), w3_b[...])

            arrived(turn, filt_in, filt_recv)
            fresh = filt_in[each, :known].astype(f32)
            edge_o[: known * each, :] = fresh.reshape(known * each, LANES)
            for e in range(each):
                ends = edge_o[pl.ds(e, count, stride=each), :]
                conv = []
                for now, taps in zip((ends, pltpu.roll(ends, LANES - 8, 1)), held[e]):
                    conv.append(short(now, jnp.where(row[:count] == 0, 0.0, pltpu.roll(now, 1, 0)), taps))
                heads[e, pl.ds(0, count, stride=pieces), :] = conv[0] * conv[1]
            spec_h[: each * rows] = forward([signal(filt_in, e).astype(bf16) for e in range(each)])
            arrived(turn, mix_in, mix_recv)
            start = (column < 2) & (lax.rem(row, pieces) == 0)
            mixes = [jnp.where(start, heads[e, :rows], signal(mix_in, e)).astype(bf16) for e in range(each)]
            spec = forward(mixes)
            prods = []
            for e in range(each):
                x, h = spec[e * rows : (e + 1) * rows], spec_h[e * rows : (e + 1) * rows]
                xr, xi, hr, hi = x[:, :LANES], x[:, LANES:], h[:, :LANES], h[:, LANES:]
                prods.append(jnp.concatenate([xr * hr - xi * hi, xr * hi + xi * hr], 1).astype(bf16))
            inv = dot(jnp.concatenate(prods, 0), w4_b[...])
            untwist = []
            for e in range(each):
                part = inv[e * rows : (e + 1) * rows]
                re, im = part[:, :LANES], part[:, LANES:]
                untwist.append(jnp.concatenate([re * tr + im * ti, im * tr - re * ti], 0).astype(bf16))
            untwisted = jnp.concatenate(untwist, 1)

            def finish(firsts):
                some = [slice(a * pieces, (a + ROW // 2) * pieces) for a in firsts]
                long_out = dot(jnp.concatenate([last[x] for x in some], 0), untwisted)
                for e in range(each):
                    mixed = jnp.concatenate([mixes[e][x] for x in some], 0).astype(f32)
                    total = long_out[:, tile(e)] + gain_s[mine * each + e] * mixed
                    total = total.reshape(len(some) * (ROW // 2), pieces, LANES).astype(bf16)
                    for i, a in enumerate(firsts):
                        reply_v[turn, e, a : a + ROW // 2] = total[i * (ROW // 2) : (i + 1) * (ROW // 2)]

            near, far, late = range(ROW // 4), range(ROW // 4, ROW // 2), range(ROW // 2, ROW)
            finish([g * ROW for g in asked[turn]])
            answer([(turn, p, g) for p in near for g in asked[turn]])
            if turn == 0:
                answer([(0, p, g) for p in far for g in asked[0]])
            if turn == 2:
                answer([(t, p, g) for p in far for t in (1, 2) for g in asked[t]])
                finish([g * ROW + ROW // 2 for g in range(groups)])
                answer([(2, p, g) for p in late for g in range(groups)])

            @pl.when((group >= asked[turn].start) & (group < asked[turn].stop))
            def _():
                back[pl.ds(mine * each, each)] = reply_v[turn, :, me]

        others = back.at[pl.ds(0, chans - each)]
        pltpu.make_async_copy(others, others, recv2_sem).wait()

    @pl.when(jnp.logical_not(holder))
    def _():
        pltpu.make_async_copy(back, back, recv2_sem).wait()

    back_f[...] = back[...].astype(f32).reshape(chans * pieces, LANES)
    for r in range(pieces):
        long_out = back_f[pl.ds(r, chans, stride=pieces), :]
        out[:, tile(r)] = (query_v[:, tile(r)] * long_out).astype(bf16)

    @pl.when(after < blocks)
    def _():
        edge.wait_send()

    sends = ((filt_m, filt_send), (mix_m, mix_send))

    @pl.when(holder)
    def _():
        for src, sem in sends:
            sent = src.at[pl.ds(0, src.shape[0] // homes * (homes - 1))]
            pltpu.make_async_copy(sent, sent, sem).wait()
        sent = reply_v.at[0, :, pl.ds(0, blocks - 1)]
        pltpu.make_async_copy(sent, sent, send2_sem).wait()

    @pl.when(jnp.logical_not(holder))
    def _():
        for src, sem in sends:
            pltpu.make_async_copy(src, src, sem).wait()


def shards(blocks, projections, short_weight, long_filter, skip_gain):
    _, chans, tokens = projections.shape
    pieces = tokens // LANES
    each = chans // (blocks // ROW * 2 * COUNT)
    rows = blocks * pieces
    consts = [jnp.asarray(x) for x in tables(blocks, pieces) + tables(blocks // 2, pieces)[:3]]
    weight = jnp.transpose(short_weight, (0, 2, 1))
    dma = pltpu.SemaphoreType.DMA
    scratch = [
        pltpu.VMEM(projections.shape, bf16),
        pltpu.VMEM(long_filter.shape, bf16),
        pltpu.VMEM(weight.shape, f32),
        pltpu.SMEM(skip_gain.shape, f32),
        *[pltpu.VMEM(x.shape, x.dtype) for x in consts],
        *[pltpu.VMEM(consts[i].shape, bf16) for i in (0, 1, 3, 4, 5, 6)],
        pltpu.VMEM((chans, LANES), bf16),
        pltpu.VMEM((16, LANES), f32),
        pltpu.VMEM((chans, tokens), f32),
        pltpu.VMEM((chans * pieces, LANES), f32),
        pltpu.VMEM((chans * pieces, LANES), f32),
        pltpu.VMEM((chans // each * (each + 1), pieces, LANES), bf16),
        pltpu.VMEM((chans, pieces, LANES), bf16),
        pltpu.VMEM((each + 1, blocks, pieces, LANES), bf16),
        pltpu.VMEM((each, blocks, pieces, LANES), bf16),
        pltpu.VMEM((blocks * each, LANES), f32),
        pltpu.VMEM((each, rows, LANES), f32),
        pltpu.VMEM((each * rows, 2 * LANES), f32),
        pltpu.VMEM((3, each, blocks, pieces, LANES), bf16),
        pltpu.VMEM((chans, pieces, LANES), bf16),
        pltpu.VMEM((chans * pieces, LANES), f32),
        dma((6,)), dma((8,)), pltpu.SemaphoreType.REGULAR, dma, dma, *[dma, dma((3,))] * 2, dma, dma,
    ]
    return pl.pallas_call(
        functools.partial(kernel, blocks),
        out_shape=pltpu.VMEM((chans, tokens), bf16),
        in_specs=[pl.BlockSpec(memory_space=pl.ANY)] * 12,
        out_specs=pl.BlockSpec(memory_space=pltpu.VMEM),
        scratch_shapes=scratch,
        compiler_params=pltpu.CompilerParams(
            collective_id=0, has_side_effects=True, vmem_limit_bytes=56 * 1024 * 1024
        ),
        cost_estimate=pl.CostEstimate(flops=200_000_000, bytes_accessed=2_000_000, transcendentals=0),
        name="hyena",
    )(projections, weight, long_filter, skip_gain, *consts)


def solution(mesh):
    in_specs = (P(None, "chan", "seq"), P(None, "chan", None), P("chan", "seq"), P("chan"))
    out_specs = P("chan", "seq")
    body = functools.partial(shards, mesh.shape["seq"])
    return jax.shard_map(body, mesh=mesh, in_specs=in_specs, out_specs=out_specs, check_vma=False)
```

```python
import functools

import jax
import jax.numpy as jnp
import numpy as np
from jax import lax
from jax.experimental import pallas as pl
from jax.experimental.pallas import tpu as pltpu
from jax.sharding import PartitionSpec as P

MESH = pl.DeviceIdType.MESH
LANES = 128
ROW = 16
FIRST, COUNT = 1, 1
GREET = (0, 2, 3, 1, 4, 5, 6, 7)
f32 = jnp.float32
bf16 = jnp.bfloat16


def tables(blocks, pieces):
    rows = blocks * pieces
    n = rows * LANES
    k1 = np.arange(rows) + 0.25
    first = np.exp(-2j * np.pi * np.outer(k1, np.arange(rows)) / rows)
    turn = np.exp(-2j * np.pi * np.outer(k1, np.arange(LANES)) / n)
    second = np.exp(-2j * np.pi * np.outer(np.arange(LANES), np.arange(LANES)) / LANES)
    back = np.conj(second)
    last = np.conj(first).T / n
    w1 = np.concatenate([first.real, first.imag], 0)
    w3 = np.block([[second.real, second.imag], [-second.imag, second.real]])
    w4 = np.block([[back.real, back.imag], [-back.imag, back.real]])
    w6 = np.concatenate([last.real, -last.imag], 1)
    tw = np.stack([turn.real, turn.imag])
    return tuple(x.astype(np.float32) for x in (w1, w6, tw, w3, w4))


def dot(a, b):
    return jnp.dot(a, b, preferred_element_type=f32)


def kernel(
    blocks, proj, weight, filt, gain, w1, w6, tw, w3, w4, w1_half, w6_half, tw_half, out,
    proj_v, filt_v, weight_v, gain_s, w1_v, w6_v, tw_v, w3_v, w4_v, w1_half_v, w6_half_v, tw_half_v,
    w1_b, w6_b, w3_b, w4_b, w1_half_b, w6_half_b,
    halo, taps_v, query_v, filt_s, mix_s, filt_m, mix_m, filt_in, mix_in, edge_o, heads, spec_h,
    reply_v, back, back_f,
    load_sem, const_sem, ready, halo_send, halo_recv, filt_send, filt_recv, mix_send, mix_recv,
    send2_sem, recv2_sem,
):
    chans = proj.shape[1]
    pieces = proj.shape[2] // LANES
    me = lax.axis_index("seq")
    groups = blocks // ROW
    homes = groups * 2 * COUNT
    each = chans // homes
    group, place = me // ROW, lax.rem(me, ROW)

    far_first = [lax.rem(group + step, groups) for step in (2, 1, 3, 0)[-groups:]]

    def holds(seq):
        chip = lax.rem(seq, ROW) // 2 - FIRST
        return (chip >= 0) & (chip < COUNT)

    holder = holds(me)
    mine = group * (2 * COUNT) + jnp.where(holder, place - 2 * FIRST, 0)

    def tile(r):
        return slice(LANES * r, LANES * (r + 1))

    loads = [
        pltpu.make_async_copy(src, dst, load_sem.at[i])
        for i, (src, dst) in enumerate(
            [(weight, weight_v), (filt, filt_v), (proj.at[1], proj_v.at[1]), (proj.at[2], proj_v.at[2])]
            + [(proj.at[0], proj_v.at[0]), (gain, gain_s)]
        )
    ]
    for load in loads:
        load.start()
    consts = [
        pltpu.make_async_copy(src, dst, const_sem.at[i])
        for i, (src, dst) in enumerate(
            [(w1, w1_v), (w6, w6_v), (tw, tw_v), (w3, w3_v), (w4, w4_v)]
            + [(w1_half, w1_half_v), (w6_half, w6_half_v), (tw_half, tw_half_v)]
        )
    ]

    barrier = pltpu.get_barrier_semaphore()

    @pl.when(holder)
    def _():
        for place_to in [2 * z + c for z in GREET for c in (0, 1)]:
            for g in far_first:
                a = g * ROW + place_to

                @pl.when(a != me)
                def _():
                    pl.semaphore_signal(barrier, inc=1, device_id={"seq": a}, device_id_type=MESH)

    after = me + 1
    bare = jnp.logical_not(holder)
    next_bare = (after < blocks) & jnp.logical_not(holds(after))
    last_bare = (me > 0) & jnp.logical_not(holds(me - 1))
    row_start, row_end = place == 0, place == ROW - 1

    @pl.when(bare & next_bare & jnp.logical_not(row_end))
    def _():
        pl.semaphore_signal(barrier, inc=1, device_id={"seq": after}, device_id_type=MESH)

    @pl.when(bare & row_start & (me > 0))
    def _():
        pl.semaphore_signal(barrier, inc=1, device_id={"seq": me - 1}, device_id_type=MESH)

    @pl.when(holder)
    def _():
        for const in consts:
            const.start()

    @pl.when(me == 0)
    def _():
        halo[...] = jnp.zeros_like(halo)

    greeted = [bare & last_bare & jnp.logical_not(row_start), next_bare & row_end]
    pl.semaphore_wait(barrier, homes - holder.astype(jnp.int32) + sum(x.astype(jnp.int32) for x in greeted))

    @pl.when(bare & jnp.logical_not(row_start))
    def _():
        pl.semaphore_signal(ready, inc=1, device_id={"seq": me - 1}, device_id_type=MESH)

    half = groups // 2
    ends_at = (ROW // 2, half * ROW - ROW // 2, blocks)
    counts = [b - a for a, b in zip((0, *ends_at), ends_at)]
    turn_of = sum((me >= b).astype(jnp.int32) for b in ends_at[:-1])
    asked = [range(1), range(1, half), range(half, groups)]

    def send(src, dst, send_sem, recv_sem):
        step = src.shape[0] // homes

        for g in far_first:
            for k in range(2 * COUNT):
                slot = jnp.where(place >= ROW * 3 // 4, 2 * COUNT - 1 - k, k)
                h, to = g * (2 * COUNT) + slot, g * ROW + 2 * FIRST + slot
                part = src.at[pl.ds(h * step, step)]

                @pl.when(to != me)
                def _():
                    pltpu.make_async_remote_copy(
                        src_ref=part,
                        dst_ref=dst.at[:, me],
                        send_sem=send_sem,
                        recv_sem=recv_sem.at[turn_of],
                        device_id={"seq": to},
                        device_id_type=MESH,
                    ).start()

        @pl.when(holder)
        def _():
            pltpu.make_async_copy(src.at[pl.ds(mine * step, step)], dst.at[:, me], recv_sem.at[turn_of]).start()

    lane = lax.broadcasted_iota(jnp.int32, (blocks, LANES), 1)

    def short(now, before, taps):
        one = pltpu.roll(jnp.where(lane[: now.shape[0]] >= LANES - 1, before, now), 1, 1)
        two = pltpu.roll(jnp.where(lane[: now.shape[0]] >= LANES - 2, before, now), 2, 1)
        total = taps[0] * two
        total = total + taps[1] * one
        total = total + taps[2] * now
        return total.astype(bf16).astype(f32)

    loads[0].wait()
    for j in range(3):
        taps_v[3 * j : 3 * j + 3, :chans] = weight_v[j]
    taps_t = taps_v[...].T[:chans]
    taps = [[taps_t[:, 3 * j + i : 3 * j + i + 1] for i in range(3)] for j in range(3)]

    loads[2].wait()
    loads[3].wait()
    here = lane[:chans]
    ends = []
    for j in (1, 2):
        head, tail = proj_v[j, :, tile(0)].astype(f32), proj_v[j, :, tile(pieces - 1)].astype(f32)
        ends.append(jnp.where(here < LANES // 2, head, tail))
    ends = jnp.where((here >= 6) & (here < 10), pltpu.roll(ends[1], 8, 1), ends[0])

    loads[1].wait()
    for r in range(pieces):
        filt_s[pl.ds(r, chans, stride=pieces), :] = filt_v[:, tile(r)].astype(f32)
    parts = [filt_s[...].reshape(homes, each, pieces, LANES), ends.reshape(homes, 1, each, LANES)]
    filt_m[...] = jnp.concatenate(parts, 1).reshape(filt_m.shape).astype(bf16)
    send(filt_m, filt_in, filt_send, filt_recv)


    for r in range(pieces):
        conv = []
        for j in (1, 2):
            now = proj_v[j, :, tile(r)].astype(f32)
            before = proj_v[j, :, tile(max(r - 1, 0))].astype(f32)
            conv.append(short(now, before, taps[j]))
        mix_s[pl.ds(r, chans, stride=pieces), :] = conv[0] * conv[1]
    mix_m[...] = mix_s[...].reshape(chans, pieces, LANES).astype(bf16)
    send(mix_m, mix_in, mix_send, mix_recv)

    loads[4].wait()
    edge = pltpu.make_async_remote_copy(
        src_ref=proj_v.at[0, :, pl.ds((pieces - 1) * LANES, LANES)],
        dst_ref=halo,
        send_sem=halo_send,
        recv_sem=halo_recv,
        device_id={"seq": jnp.minimum(after, blocks - 1)},
        device_id_type=MESH,
    )

    @pl.when(next_bare & jnp.logical_not(row_end))
    def _():
        pl.semaphore_wait(ready, 1)

    @pl.when(after < blocks)
    def _():
        edge.start()

    for r in reversed(range(pieces)):
        if r == 0:

            @pl.when(me > 0)
            def _():
                edge.wait_recv()

        now = proj_v[0, :, tile(r)].astype(f32)
        before = (halo[...] if r == 0 else proj_v[0, :, tile(r - 1)]).astype(f32)
        query_v[:, tile(r)] = short(now, before, taps[0])

    loads[5].wait()

    @pl.when(holder)
    def _():
        for const in consts:
            const.wait()
        for src, dst in (
            (w1_v, w1_b), (w6_v, w6_b), (w3_v, w3_b), (w4_v, w4_b), (w1_half_v, w1_half_b), (w6_half_v, w6_half_b)
        ):
            dst[...] = src[...].astype(bf16)
        edge_o[...] = jnp.zeros_like(edge_o)
        chan_lane = lax.broadcasted_iota(jnp.int32, weight_v.shape[1:], 1)
        held = []
        for e in range(each):
            here = chan_lane == mine * each + e
            rows_j = [jnp.sum(jnp.where(here, weight_v[j], 0.0), axis=1, keepdims=True) for j in (1, 2)]
            held.append([[x[i : i + 1, :] for i in range(3)] for x in rows_j])

        def arrived(turn, dst, sem):
            some = dst.at[:, pl.ds(0, counts[turn])]
            pltpu.make_async_copy(some, some, sem.at[turn]).wait()

        def answer(places):
            for turn, place_to, g in places:
                a = g * ROW + place_to

                @pl.when(me != a)
                def _():
                    pltpu.make_async_remote_copy(
                        src_ref=reply_v.at[turn, :, a],
                        dst_ref=back.at[pl.ds(mine * each, each)],
                        send_sem=send2_sem,
                        recv_sem=recv2_sem,
                        device_id={"seq": a},
                        device_id_type=MESH,
                    ).start()

        for turn, known in enumerate(ends_at):
            count = half * ROW if turn < 2 else blocks
            rows = count * pieces
            first, last, turns = (w1_half_b, w6_half_b, tw_half_v) if turn < 2 else (w1_b, w6_b, tw_v)
            tr, ti = turns[0], turns[1]
            row = lax.broadcasted_iota(jnp.int32, (rows, LANES), 0)
            column = lax.broadcasted_iota(jnp.int32, (rows, LANES), 1)

            def signal(src, e):
                got = src[e, :known].astype(f32).reshape(known * pieces, LANES)
                if known < count:
                    got = jnp.concatenate([got, jnp.zeros((rows - known * pieces, LANES), f32)], 0)
                return got

            def forward(signals, step=None):
                if step is None:
                    step = dot(first[...], jnp.concatenate(signals, 1))
                turned = []
                for e in range(len(signals)):
                    re, im = step[:rows, tile(e)], step[rows:, tile(e)]
                    turned.append(jnp.concatenate([re * tr - im * ti, re * ti + im * tr], 1).astype(bf16))
                return dot(jnp.concatenate(turned, 0), w3_b[...])

            arrived(turn, filt_in, filt_recv)
            fresh = filt_in[each, :known].astype(f32)
            edge_o[: known * each, :] = fresh.reshape(known * each, LANES)
            for e in range(each):
                ends = edge_o[pl.ds(e, count, stride=each), :]
                conv = []
                for now, taps in zip((ends, pltpu.roll(ends, LANES - 8, 1)), held[e]):
                    conv.append(short(now, jnp.where(row[:count] == 0, 0.0, pltpu.roll(now, 1, 0)), taps))
                heads[e, pl.ds(0, count, stride=pieces), :] = conv[0] * conv[1]
            spec_h[: each * rows] = forward([signal(filt_in, e).astype(bf16) for e in range(each)])
            arrived(turn, mix_in, mix_recv)
            start = (column < 2) & (lax.rem(row, pieces) == 0)
            mixes = [jnp.where(start, heads[e, :rows], signal(mix_in, e)).astype(bf16) for e in range(each)]
            pairs = [mixes[e : e + 2] for e in range(0, each, 2)]
            steps = [dot(first[...], jnp.concatenate(pair, 1)) for pair in pairs]
            spec = jnp.concatenate([forward(pair, step) for pair, step in zip(pairs, steps)], 0)
            prods = []
            for e in range(each):
                x, h = spec[e * rows : (e + 1) * rows], spec_h[e * rows : (e + 1) * rows]
                xr, xi, hr, hi = x[:, :LANES], x[:, LANES:], h[:, :LANES], h[:, LANES:]
                prods.append(jnp.concatenate([xr * hr - xi * hi, xr * hi + xi * hr], 1).astype(bf16))
            inv = jnp.concatenate(
                [dot(jnp.concatenate(prods[e : e + 2], 0), w4_b[...]) for e in range(0, each, 2)], 0
            )
            untwist = []
            for e in range(each):
                part = inv[e * rows : (e + 1) * rows]
                re, im = part[:, :LANES], part[:, LANES:]
                untwist.append(jnp.concatenate([re * tr + im * ti, im * tr - re * ti], 0).astype(bf16))
            untwisted = jnp.concatenate(untwist, 1)

            def finish(firsts):
                some = [slice(a * pieces, (a + ROW // 2) * pieces) for a in firsts]
                long_out = dot(jnp.concatenate([last[x] for x in some], 0), untwisted)
                for e in range(each):
                    mixed = jnp.concatenate([mixes[e][x] for x in some], 0).astype(f32)
                    total = long_out[:, tile(e)] + gain_s[mine * each + e] * mixed
                    total = total.reshape(len(some) * (ROW // 2), pieces, LANES).astype(bf16)
                    for i, a in enumerate(firsts):
                        reply_v[turn, e, a : a + ROW // 2] = total[i * (ROW // 2) : (i + 1) * (ROW // 2)]

            near, far, late = range(ROW // 4), range(ROW // 4, ROW // 2), range(ROW // 2, ROW)
            finish([g * ROW for g in asked[turn]])
            answer([(turn, p, g) for p in near for g in asked[turn]])
            if turn == 0:
                answer([(0, p, g) for p in far for g in asked[0]])
            if turn == 2:
                answer([(t, p, g) for p in far for t in (1, 2) for g in asked[t]])
                finish([g * ROW + ROW // 2 for g in range(groups)])
                answer([(2, p, g) for p in late for g in range(groups)])

            @pl.when((group >= asked[turn].start) & (group < asked[turn].stop))
            def _():
                back[pl.ds(mine * each, each)] = reply_v[turn, :, me]

        others = back.at[pl.ds(0, chans - each)]
        pltpu.make_async_copy(others, others, recv2_sem).wait()

    @pl.when(jnp.logical_not(holder))
    def _():
        pltpu.make_async_copy(back, back, recv2_sem).wait()

    back_f[...] = back[...].astype(f32).reshape(chans * pieces, LANES)
    for r in range(pieces):
        long_out = back_f[pl.ds(r, chans, stride=pieces), :]
        out[:, tile(r)] = (query_v[:, tile(r)] * long_out).astype(bf16)

    @pl.when(after < blocks)
    def _():
        edge.wait_send()

    sends = ((filt_m, filt_send), (mix_m, mix_send))

    @pl.when(holder)
    def _():
        for src, sem in sends:
            sent = src.at[pl.ds(0, src.shape[0] // homes * (homes - 1))]
            pltpu.make_async_copy(sent, sent, sem).wait()
        sent = reply_v.at[0, :, pl.ds(0, blocks - 1)]
        pltpu.make_async_copy(sent, sent, send2_sem).wait()

    @pl.when(jnp.logical_not(holder))
    def _():
        for src, sem in sends:
            pltpu.make_async_copy(src, src, sem).wait()


def shards(blocks, projections, short_weight, long_filter, skip_gain):
    _, chans, tokens = projections.shape
    pieces = tokens // LANES
    each = chans // (blocks // ROW * 2 * COUNT)
    rows = blocks * pieces
    consts = [jnp.asarray(x) for x in tables(blocks, pieces) + tables(blocks // 2, pieces)[:3]]
    weight = jnp.transpose(short_weight, (0, 2, 1))
    dma = pltpu.SemaphoreType.DMA
    scratch = [
        pltpu.VMEM(projections.shape, bf16),
        pltpu.VMEM(long_filter.shape, bf16),
        pltpu.VMEM(weight.shape, f32),
        pltpu.SMEM(skip_gain.shape, f32),
        *[pltpu.VMEM(x.shape, x.dtype) for x in consts],
        *[pltpu.VMEM(consts[i].shape, bf16) for i in (0, 1, 3, 4, 5, 6)],
        pltpu.VMEM((chans, LANES), bf16),
        pltpu.VMEM((16, LANES), f32),
        pltpu.VMEM((chans, tokens), f32),
        pltpu.VMEM((chans * pieces, LANES), f32),
        pltpu.VMEM((chans * pieces, LANES), f32),
        pltpu.VMEM((chans // each * (each + 1), pieces, LANES), bf16),
        pltpu.VMEM((chans, pieces, LANES), bf16),
        pltpu.VMEM((each + 1, blocks, pieces, LANES), bf16),
        pltpu.VMEM((each, blocks, pieces, LANES), bf16),
        pltpu.VMEM((blocks * each, LANES), f32),
        pltpu.VMEM((each, rows, LANES), f32),
        pltpu.VMEM((each * rows, 2 * LANES), f32),
        pltpu.VMEM((3, each, blocks, pieces, LANES), bf16),
        pltpu.VMEM((chans, pieces, LANES), bf16),
        pltpu.VMEM((chans * pieces, LANES), f32),
        dma((6,)), dma((8,)), pltpu.SemaphoreType.REGULAR, dma, dma, *[dma, dma((3,))] * 2, dma, dma,
    ]
    return pl.pallas_call(
        functools.partial(kernel, blocks),
        out_shape=pltpu.VMEM((chans, tokens), bf16),
        in_specs=[pl.BlockSpec(memory_space=pl.ANY)] * 12,
        out_specs=pl.BlockSpec(memory_space=pltpu.VMEM),
        scratch_shapes=scratch,
        compiler_params=pltpu.CompilerParams(
            collective_id=0, has_side_effects=True, vmem_limit_bytes=56 * 1024 * 1024
        ),
        cost_estimate=pl.CostEstimate(flops=200_000_000, bytes_accessed=2_000_000, transcendentals=0),
        name="hyena",
    )(projections, weight, long_filter, skip_gain, *consts)


def solution(mesh):
    in_specs = (P(None, "chan", "seq"), P(None, "chan", None), P("chan", "seq"), P("chan"))
    out_specs = P("chan", "seq")
    body = functools.partial(shards, mesh.shape["seq"])
    return jax.shard_map(body, mesh=mesh, in_specs=in_specs, out_specs=out_specs, check_vma=False)
```
